32 devices in a mesh: lon: 4 (over y, x), lat: 8 (over z, core).
Axes of the slice: x: 2, y: 2, z: 4, core: 2. Of those that a mesh axis runs over, the one named last changes fastest.
Arguments:
- sensitivity: float32 [32, 1440, 128], P('lat', 'lon'), may hold values from -6 to 6
- courant_east: float32 [32, 1440, 32], P('lat', 'lon'), may hold values from -0.9 to 0.9
- courant_north: float32 [32, 1440, 32], P('lat', 'lon'), may hold values from -0.9 to 0.9
- mixing: float32 [32, 1440, 31], P('lat', 'lon'), may hold values from 0.05 to 5
- cutoff: int32 [32], P('lat'), may hold values from 4 to 359
- polar_flag: int32 [32], P('lat'), may hold values from 0 to 1, as said below
Outputs:
- adjoint_out: float32 [32, 1440, 128], P('lat', 'lon')
The draws below stay inside these ranges and needn't reach their ends.
Inputs may be any that keep to these rules, and one draw needn't show every extreme that they name: polar_flag is 1 on a run of rows starting at row 0 and on a run ending at row 31, each of 1 to 8 rows and one of them exactly 8, and 0 elsewhere.
All inputs are finite; a program needn't handle non-finite values.
Results may differ from the reference program's by a relative error of at most 0.0003.
Values sent between devices are 32-bit elements; how exact they have to be, the bound alone decides.
No kernel may reach another device: no remote copies, remote signals or barrier semaphores. Data moves between devices by JAX's collectives and lax.ppermute only.
A program may use at most 64 MiB of HBM per device.

```python
import math
import jax
import jax.numpy as jnp
from jax import lax

NLON = 1440
TRACERS = 4
LEV = 32
SUBSTEPS = 2
LAT = 32
LEVM1 = 31
CHANNELS = 128
POLAR = 8


def draw_polar_flag(key, part):
    rows = jnp.arange(LAT, dtype=jnp.int32)
    other = jax.random.randint(key, (), 1, POLAR + 1)
    flipped = jax.random.randint(jax.random.fold_in(key, 7), (), 0, 2)
    first_count = jnp.where(flipped == 0, POLAR, other)
    second_count = jnp.where(flipped == 0, other, POLAR)
    return jnp.where((rows < first_count) | (rows >= LAT - second_count), 1, 0).astype(jnp.int32)


def set_ends(array, own_key, least, largest):
    shape = array.shape
    spot = [jax.random.randint(jax.random.fold_in(own_key, axis), (), 0, shape[axis]) for axis in range(len(shape))]
    array = array.at[tuple(spot)].set(least)
    longest = shape.index(max(shape))
    spot[longest] = (spot[longest] + 1) % shape[longest]
    return array.at[tuple(spot)].set(largest)


def level_of(key, extent, cuts, low, high):
    def one(dim, parts):
        draws = jax.random.uniform(jax.random.fold_in(jax.random.fold_in(key, 6), dim), (parts,), jnp.float32, low / len(cuts), high / len(cuts))
        return jnp.repeat(jnp.exp(draws), extent[dim] // parts).reshape((-1,) + (1,) * (len(extent) - dim - 1))

    factor_of = one(*cuts[0])
    for cut in cuts[1:]:
        factor_of = factor_of * one(*cut)
    return factor_of


def scatter_about(own_key, dims, deviation, reach, pieces=(), kind=jnp.bfloat16):
    drawn = deviation * jax.random.normal(own_key, dims, jnp.float32)
    if pieces:
        drawn = drawn * level_of(own_key, dims, pieces, -0.22, 0.18)
    return jnp.clip(drawn, -reach, reach).astype(kind)


def setup_inputs(seed: int = 0) -> dict:
    key_of = jax.random.split(jax.random.key(seed), 7)
    return {
        "sensitivity": scatter_about(key_of[0], (LAT, NLON, CHANNELS), 1.0, 6.0, ((0, 8), (1, 4)), jnp.float32),
        "courant_east": jnp.clip(jax.random.uniform(key_of[1], (LAT, NLON, LEV), jnp.float32, -0.9, 0.9) * level_of(key_of[1], (LAT, NLON, LEV), ((0, 8), (1, 4)), -0.4, 0.0), -0.9, 0.9),
        "courant_north": jnp.clip(jax.random.uniform(key_of[2], (LAT, NLON, LEV), jnp.float32, -0.9, 0.9) * level_of(key_of[2], (LAT, NLON, LEV), ((0, 8), (1, 4)), -0.4, 0.0), -0.9, 0.9),
        "mixing": jnp.clip(jnp.exp(math.log(5.0) - 4.6051702 * jax.random.uniform(key_of[3], (LAT, NLON, LEVM1), jnp.float32) ** level_of(key_of[3], (LAT, NLON, LEVM1), ((0, 8), (1, 4)), -0.2, 0.2)), 0.05, 5.0),
        "cutoff": set_ends(jax.random.randint(key_of[4], (LAT,), 4, NLON // 4), jax.random.fold_in(key_of[4], 1), 4, (NLON // 4) - 1).astype(jnp.int32),
        "polar_flag": draw_polar_flag(jax.random.fold_in(key_of[6], 71), 0),
    }


def edge_row(offset):
    row = [0.0] * 6
    row[offset + 2] += 7.0 / 12.0
    row[offset + 3] += 7.0 / 12.0
    row[offset + 1] -= 1.0 / 12.0
    row[offset + 4] -= 1.0 / 12.0
    return row


def flux_weights(courant):
    left_edge = edge_row(-1)
    middle_edge = edge_row(0)
    right_edge = edge_row(1)
    magnitude = jnp.abs(courant)
    result = []
    for position in range(6):
        cell_plus = 1.0 if position == 2 else 0.0
        cell_minus = 1.0 if position == 3 else 0.0
        delta_plus = middle_edge[position] - left_edge[position]
        curve_plus = 6.0 * (cell_plus - 0.5 * (left_edge[position] + middle_edge[position]))
        delta_minus = right_edge[position] - middle_edge[position]
        curve_minus = 6.0 * (cell_minus - 0.5 * (middle_edge[position] + right_edge[position]))
        bend = 1.0 - 2.0 * magnitude / 3.0
        forward_weight = middle_edge[position] - 0.5 * magnitude * (delta_plus - bend * curve_plus)
        backward_weight = middle_edge[position] + 0.5 * magnitude * (delta_minus + bend * curve_minus)
        result.append(courant * jnp.where(courant >= 0.0, forward_weight, backward_weight))
    return result


def spread_flux(field_ext, courant_ext, axis_dim):
    length = field_ext.shape[axis_dim]
    jump = lax.slice_in_dim(field_ext, 1, length, axis=axis_dim) - lax.slice_in_dim(field_ext, 0, length - 1, axis=axis_dim)
    weights = flux_weights(lax.slice_in_dim(courant_ext, 0, length - 1, axis=axis_dim))
    padding = [(0, 0)] * jump.ndim
    padding[axis_dim] = (3, 3)
    total = jnp.zeros(field_ext.shape, field_ext.dtype)
    for position in range(6):
        offset = position - 2
        term = jnp.pad(weights[position] * jump, padding)
        total = total + lax.slice_in_dim(term, 3 - offset, 3 - offset + length, axis=axis_dim)
    return total


def vertical_solve(field, mixing):
    rows, cols, channels = field.shape
    levels = mixing.shape[2] + 1
    stack = jnp.moveaxis(field.reshape(rows, cols, levels, channels // levels), 2, 0)
    coef = jnp.moveaxis(mixing, 2, 0)
    nothing = jnp.zeros_like(coef[:1])
    padded = jnp.concatenate([nothing, coef, nothing], axis=0)
    beneath = -padded[:levels]
    overlying = -padded[1:]
    central = 1.0 - beneath - overlying

    def forward(previous, inputs):
        factor_prev, partial_prev = previous
        below_coef, above_coef, centre_coef, source = inputs
        divisor = centre_coef - below_coef * factor_prev
        factor = above_coef / divisor
        partial_now = (source - below_coef[..., None] * partial_prev) / divisor[..., None]
        return (factor, partial_now), (factor, partial_now)

    start = (jnp.zeros_like(coef[0]), jnp.zeros_like(stack[0]))
    unused, (factors, partials) = lax.scan(forward, start, (beneath, overlying, central, stack))

    def backward(following, inputs):
        factor, partial_now = inputs
        current = partial_now - factor[..., None] * following
        return current, current

    unused, solved = lax.scan(backward, jnp.zeros_like(stack[0]), (factors, partials), reverse=True)
    return jnp.moveaxis(solved, 0, 2).reshape(rows, cols, channels)


def polar_filter(field, cutoff, polar_flag):
    spectra = jnp.fft.rfft(field, axis=1)
    waves = jnp.arange(spectra.shape[1], dtype=jnp.int32)
    keeping = waves[None, :] <= cutoff[:, None]
    filtered = jnp.fft.irfft(jnp.where(keeping[:, :, None], spectra, 0.0), n=field.shape[1], axis=1).astype(field.dtype)
    return jnp.where((polar_flag > 0)[:, None, None], filtered, field)


def meridional_adjoint(field, courant_north):
    rows_total = field.shape[0]
    rows = jnp.arange(rows_total, dtype=jnp.int32)
    masked = jnp.where((rows < rows_total - 1)[:, None, None], courant_north, 0.0)
    courant = jnp.repeat(masked, TRACERS, axis=2)
    field_ext = jnp.pad(field, ((3, 3), (0, 0), (0, 0)))
    courant_ext = jnp.pad(courant, ((3, 3), (0, 0), (0, 0)))
    full = spread_flux(field_ext, courant_ext, 0)
    result = field + full[3:3 + rows_total]
    halfway = field.shape[1] // 2
    south = jnp.roll(full[0:3], halfway, axis=1)[::-1]
    north = jnp.roll(full[rows_total + 3:rows_total + 6], halfway, axis=1)[::-1]
    result = result.at[0:3].add(south)
    result = result.at[rows_total - 3:].add(north)
    return result


def zonal_adjoint(field, courant_east):
    circle = field.shape[1]
    field_ext = jnp.concatenate([field[:, circle - 3:], field, field[:, :3]], axis=1)
    courant = jnp.repeat(courant_east, TRACERS, axis=2)
    courant_ext = jnp.concatenate([courant[:, circle - 3:], courant, courant[:, :3]], axis=1)
    return field + spread_flux(field_ext, courant_ext, 1)[:, 3:3 + circle]


def reference(sensitivity, courant_east, courant_north, mixing, cutoff, polar_flag):
    state = sensitivity
    for substep in range(SUBSTEPS):
        state = vertical_solve(state, mixing)
        state = polar_filter(state, cutoff, polar_flag)
        state = meridional_adjoint(state, courant_north)
        state = zonal_adjoint(state, courant_east)
    return state
```

```python
from functools import partial
import math

import jax
import jax.numpy as jnp
import ml_dtypes
import numpy as np
from jax import lax
from jax.experimental import pallas as pl
from jax.experimental.pallas import tpu as pltpu
from jax.sharding import PartitionSpec as P

SUBSTEPS = 2
QUARTERS = 4
HALO = 3
SUB = 8
f32 = jnp.float32
bf16 = jnp.bfloat16


def round_up(n, k):
    return -(-n // k) * k


def fourier_tables(nlon, wide):
    quarter = nlon // 4
    top = nlon // 4 - 1
    even = list(range(0, top + 1, 2))
    odd = list(range(1, top + 1, 2))
    width = round_up(2 * max(len(even), len(odd)), 128)
    x = np.arange(2 * quarter)
    place = (x // quarter) * wide + x % quarter
    result = []
    for waves in (even, odd):
        k = np.array(waves, np.int64)
        angle = (x[:, None] * k[None, :] % nlon) * (2.0 * math.pi / nlon)
        scale = np.where(k == 0, 1.0, 2.0) / nlon
        ahead = np.zeros((2 * wide, width))
        back = np.zeros((width, 2 * wide))
        index = np.full((1, width), nlon, np.int32)
        n = len(waves)
        ahead[place, :n] = np.cos(angle)
        ahead[place, n : 2 * n] = np.sin(angle)
        back[:n, place] = (np.cos(angle) * scale).T
        back[n : 2 * n, place] = (np.sin(angle) * scale).T
        index[0, :n] = k
        index[0, n : 2 * n] = k
        parts = []
        for table in (ahead, back):
            high = table.astype(np.float32).astype(ml_dtypes.bfloat16)
            low = (table - high.astype(np.float64)).astype(np.float32).astype(ml_dtypes.bfloat16)
            parts += [high, low]
        result += parts + [index]
    return result


def split(x):
    high = x.astype(bf16)
    return high, (x - high.astype(f32)).astype(bf16)


def product(high, low, t_high, t_low):
    total = jnp.dot(high, t_high, preferred_element_type=f32)
    total = total + jnp.dot(low, t_high, preferred_element_type=f32)
    return total + jnp.dot(high, t_low, preferred_element_type=f32)


def column_factors(mix_at, levels, shape, store):
    zero = jnp.zeros(shape, f32)
    h_before = zero
    below = zero
    for level in range(levels):
        above = mix_at(level) if level < levels - 1 else zero
        divisor = 1.0 + below + above - below * h_before
        g = 1.0 / divisor
        h = above * g
        store(level, g, below * g, h)
        h_before = h
        below = above


def column_solve(v, g, a, h):
    n = len(v)
    y = [g[0] * v[0]]
    carry = [a[0]]
    for q in range(1, n):
        y.append(g[q] * v[q] + a[q] * y[q - 1])
        carry.append(a[q] * carry[q - 1])
    z, p = y[n - 1], carry[n - 1]
    step = 1
    while step < SUB:
        z = z + p * pltpu.roll(z, step, 0)
        if 2 * step < SUB:
            p = p * pltpu.roll(p, step, 0)
        step *= 2
    before = pltpu.roll(z, 1, 0)
    y = [y[q] + carry[q] * before for q in range(n - 1)] + [z]
    x = [None] * n
    back = [None] * n
    x[n - 1] = y[n - 1]
    back[n - 1] = h[n - 1]
    for q in range(n - 2, -1, -1):
        x[q] = y[q] + h[q] * x[q + 1]
        back[q] = h[q] * back[q + 1]
    z, p = x[0], back[0]
    step = 1
    while step < SUB:
        z = z + p * pltpu.roll(z, SUB - step, 0)
        if 2 * step < SUB:
            p = p * pltpu.roll(p, SUB - step, 0)
        step *= 2
    after = pltpu.roll(z, SUB - 1, 0)
    return [z] + [x[q] + back[q] * after for q in range(1, n)]


def put(ref, at, value):
    for c in range(ref.shape[0]):
        n = min(128, value.shape[1] - c * 128)
        ref[c, at, :n] = value[:, c * 128 : c * 128 + n]


def get(ref, at):
    return jnp.concatenate([ref[c, at, :] for c in range(ref.shape[0])], axis=1)


def clear(*refs):
    for ref in refs:
        ref[...] = jnp.zeros(ref.shape, f32)


def factor_scratch(rows, levels, wide):
    return [(wide // 128, rows * levels, 128)] * 3


def first_solve_kernel(tiles, order, sens, mix, *refs):
    rows, width, channels = sens.shape
    levels = mix.shape[0] + 1
    tracers = channels // levels
    outs = refs[:tracers]
    turned, mixed, g_s, a_s, h_s = refs[tracers:]
    wide = mixed.shape[2]
    if wide != width:
        clear(turned, mixed)
    mixed[:, :, :width] = mix[...]

    def store(level, g, a, h):
        at = pl.ds((level % tiles) * SUB + level // tiles, rows, stride=levels)
        for s, value in ((g_s, g), (a_s, a), (h_s, h)):
            put(s, at, value)

    column_factors(lambda l: mixed[l], levels, (rows, wide), store)
    for r in range(rows):
        put(turned, slice(0, channels), sens[r].T)
        at = lambda q: slice(r * levels + q * SUB, r * levels + q * SUB + SUB)
        g, a, h = ([get(s, at(q)) for q in range(tiles)] for s in (g_s, a_s, h_s))
        for j in range(tracers):
            t = order[j]
            v = [get(turned, pl.ds(q * tracers + t, SUB, stride=tiles * tracers)) for q in range(tiles)]
            x = column_solve(v, g, a, h)
            for q in range(tiles):
                outs[j][r, q] = x[q]


def pack_rows(src, turned, tiles, emit):
    rows, levels, width = src.shape
    for r in range(rows):
        put(turned, slice(r * levels, (r + 1) * levels), src[r])
    for r in range(rows):
        for q in range(tiles):
            emit(r, q, get(turned, pl.ds(r * levels + q, SUB, stride=tiles)))


def pack_levels_kernel(tiles, src, out, turned):
    clear(turned)

    def emit(r, q, value):
        out[r, q] = value

    pack_rows(src, turned, tiles, emit)


def pack_both_kernel(tiles, src, mix, out, turned):
    rows, levels, width = src.shape
    clear(turned)
    out[1] = jnp.zeros(out.shape[1:], f32)

    def emit(r, q, value):
        out[0, r * tiles + q] = value

    pack_rows(src, turned, tiles, emit)
    per = SUB // rows
    for level in range(levels - 1):
        at = level % per * rows
        out[1, level // per, at : at + rows, :width] = mix[level]


def unpack_kernel(tiles, order, *refs):
    n = len(refs) - 2
    pieces, out, turned = refs[:n], refs[n], refs[n + 1]
    rows, width, channels = out.shape
    for r in range(rows):
        for j in range(n):
            t = order[j]
            for q in range(tiles):
                put(turned, pl.ds(q * n + t, SUB, stride=tiles * n), pieces[j][r, q])
        out[r] = get(turned, slice(0, channels))[:, :width].T


def filter_block(field, tables, cut, flag, emit):
    rows, groups, sub, wide = field.shape
    tiles = groups // QUARTERS
    levels = tiles * sub
    quarter = [
        field[:, q * tiles : (q + 1) * tiles].reshape(rows * levels, wide) for q in range(QUARTERS)
    ]
    halves = []
    for sign in (0, 1):
        ahead_h, ahead_l, back_h, back_l, index = tables[5 * sign : 5 * sign + 5]
        if sign:
            pair = [quarter[0] - quarter[2], quarter[1] - quarter[3]]
        else:
            pair = [quarter[0] + quarter[2], quarter[1] + quarter[3]]
        high, low = split(jnp.concatenate(pair, axis=1))
        spectrum = product(high, low, ahead_h[...], ahead_l[...])
        kept = [
            jnp.where(index[...] <= cut(r), spectrum[r * levels : (r + 1) * levels], 0.0)
            for r in range(rows)
        ]
        high, low = split(jnp.concatenate(kept, axis=0))
        halves.append(product(high, low, back_h[...], back_l[...]))
    even, odd = halves
    for r in range(rows):
        at = slice(r * levels, (r + 1) * levels)
        for q in range(QUARTERS):
            lanes = slice((q % 2) * wide, (q % 2 + 1) * wide)
            e, o = even[at, lanes], odd[at, lanes]
            smooth = e + o if q < 2 else e - o
            emit(r, q, jnp.where(flag(r) > 0, smooth, quarter[q][at]))


def filter_and_edges(field, tables, info, out, edge_z, edge_c):
    rows, groups, sub, wide = field.shape
    tiles = groups // QUARTERS
    cut = lambda r: info[8 + r]
    flag = lambda r: info[8 + rows + r]
    active = flag(0)
    for r in range(1, rows):
        active = active | flag(r)

    @pl.when(active > 0)
    def _():
        def emit(r, q, value):
            out[r, q * tiles : (q + 1) * tiles] = value.reshape(tiles, sub, wide)

        filter_block(field, tables, cut, flag, emit)

    @pl.when(active == 0)
    def _():
        out[...] = field[...]

    write_edges(out, info, edge_z, edge_c)


def write_edges(field, info, edge_z, edge_c):
    shift = field.shape[0] - HALO
    odd = info[4]
    edge_z[...] = field[pl.ds(odd * shift, HALO)]
    edge_c[...] = field[pl.ds((1 - odd) * shift, HALO)]


def place_halo(info, halo, from_z, from_c):
    odd = info[4]
    halo[pl.ds(odd * HALO, HALO)] = from_z[...]
    halo[pl.ds((1 - odd) * HALO, HALO)] = from_c[...]


def flux_terms(courant, jump):
    size = jnp.abs(courant)
    rest = 1.0 - size
    carried = courant * jump
    t = carried * rest
    edge = t * rest
    upwind = -(t * size)
    cell = carried * size * (3.0 - 2.0 * size)
    ahead = courant >= 0.0
    up_plus = jnp.where(ahead, upwind, 0.0)
    cell_plus = jnp.where(ahead, cell, 0.0)
    return edge, up_plus, upwind - up_plus, cell_plus, cell - cell_plus


def meridional_pass(field, halo, north, north_halo, ghosts, out):
    rows, groups, sub, wide = field.shape

    def body(i, _):
        def value(g):
            if g < 0:
                return halo[g + HALO, i]
            return field[g, i] if g < rows else halo[HALO + g - rows, i]

        def courant(g):
            if g < 0:
                return north_halo[g + HALO, i]
            return north[g, i] if g < rows else north_halo[HALO + g - rows, i]

        edge = {}
        cell = {}

        def add(store, at, x, low, high):
            if low <= at <= high:
                store[at] = store[at] + x if at in store else x

        below = value(-HALO)
        for f in range(-HALO, rows + 2):
            above = value(f + 1)
            e, up_plus, up_minus, cell_plus, cell_minus = flux_terms(courant(f), above - below)
            add(edge, f, e, -2, rows)
            add(edge, f - 1, up_plus, -2, rows)
            add(edge, f + 1, up_minus, -2, rows)
            add(cell, f, cell_plus, 0, rows - 1)
            add(cell, f + 1, cell_minus, 0, rows - 1)
            below = above
        for r in range(rows):
            near = edge[r] + edge[r - 1]
            far = edge[r + 1] + edge[r - 2]
            out[r, i] = value(r) + cell[r] + (7.0 / 12.0) * near - (1.0 / 12.0) * far
        ghosts[0, i] = (7.0 / 12.0) * edge[-1] - (1.0 / 12.0) * edge[0]
        ghosts[1, i] = (-1.0 / 12.0) * edge[-1]
        ghosts[2, i] = (7.0 / 12.0) * edge[rows - 1] - (1.0 / 12.0) * edge[rows - 2]
        ghosts[3, i] = (-1.0 / 12.0) * edge[rows - 1]
        return 0

    lax.fori_loop(0, groups, body, 0)


def pole_pass(info, ghosts, out):
    rows, groups, sub, wide = out.shape
    half = groups // 2
    for flag_at, targets in ((5, ((0, 0), (1, 1))), (6, ((2, rows - 1), (3, rows - 2)))):

        @pl.when(info[flag_at] > 0)
        def _():
            for ghost, row in targets:
                out[row, :half] = out[row, :half] + ghosts[ghost, half:]
                out[row, half:] = out[row, half:] + ghosts[ghost, :half]


def widen(values, width):
    wide = values[0].shape[1]
    lane = lax.broadcasted_iota(jnp.int32, values[0].shape, 1)
    result = []
    for q in range(QUARTERS):
        after = pltpu.roll(values[(q + 1) % QUARTERS], width, 1)
        before = pltpu.roll(values[(q - 1) % QUARTERS], wide - width, 1)
        padded = jnp.where(lane < width + HALO, after, before)
        padded = jnp.where((lane >= width + HALO) & (lane < wide - HALO), 0.0, padded)
        result.append(jnp.where(lane < width, values[q], padded))
    return result


def zonal_block(value, courant):
    wide = value.shape[1]
    left = lambda x: pltpu.roll(x, wide - 1, 1)
    right = lambda x: pltpu.roll(x, 1, 1)
    edge, up_plus, up_minus, cell_plus, cell_minus = flux_terms(courant, left(value) - value)
    edge = edge + left(up_plus) + right(up_minus)
    pair = edge + right(edge)
    twelfth = (1.0 / 12.0) * pair
    return value + cell_plus + 8.0 * twelfth - left(twelfth) + right(cell_minus - twelfth)


def zonal_pass(width, field, east, emit):
    rows, groups, sub, wide = field.shape
    tiles = groups // QUARTERS

    def body(i, _):
        r, tile = i // tiles, i % tiles
        values = widen([field[r, q * tiles + tile] for q in range(QUARTERS)], width)
        for q in range(QUARTERS):
            emit(r, q, tile, zonal_block(values[q], east[r, q * tiles + tile]))
        return 0

    lax.fori_loop(0, rows * tiles, body, 0)


def solve_pass(field, g, a, h):
    rows, groups, sub, wide = field.shape
    tiles = groups // QUARTERS

    def body(i, _):
        r, q = i // QUARTERS, i % QUARTERS
        take = lambda ref: [ref[r, q * tiles + tile] for tile in range(tiles)]
        x = column_solve(take(field), take(g), take(a), take(h))
        for tile in range(tiles):
            field[r, q * tiles + tile] = x[tile]
        return 0

    lax.fori_loop(0, rows * QUARTERS, body, 0)


def first_filter_kernel(tiles, info, *refs):
    pieces, tables = refs[:4], refs[4:14]
    out, edge_z, edge_c, field = refs[14:]
    for j in range(QUARTERS):
        field[:, pl.ds(info[j] * tiles, tiles)] = pieces[j][...]
    filter_and_edges(field, tables, info, out, edge_z, edge_c)


def north_kernel(tiles, info, *refs):
    pieces = refs[:4]
    out, edge_z, edge_c = refs[4:]
    rows = out.shape[0]
    for j in range(QUARTERS):
        out[:, pl.ds(info[j] * tiles, tiles)] = pieces[j][...]

    @pl.when(info[6] > 0)
    def _():
        out[rows - 1] = jnp.zeros(out.shape[1:], f32)

    write_edges(out, info, edge_z, edge_c)


def coefficient_kernel(tiles, width, info, *refs):
    pieces = refs[:4]
    east, g_o, a_o, h_o, raw, g_s, a_s, h_s = refs[4:]
    rows, groups, sub, wide = east.shape
    levels = tiles * sub
    per = SUB // rows
    for j in range(QUARTERS):
        q = info[j]
        for r in range(rows):
            raw[r, pl.ds(q * tiles, tiles)] = pieces[j][0, r * tiles : (r + 1) * tiles]

        def store(level, g, a, h):
            at = (level % tiles) * SUB + level // tiles
            for s, value in ((g_s, g), (a_s, a), (h_s, h)):
                put(s, pl.ds(at, rows, stride=levels), value)

        mix_at = lambda l: pieces[j][1, l // per, l % per * rows : l % per * rows + rows, :]
        column_factors(mix_at, levels, (rows, wide), store)
        for s, o in ((g_s, g_o), (a_s, a_o), (h_s, h_o)):
            o[:, pl.ds(q * tiles, tiles)] = get(s, slice(0, rows * levels)).reshape(rows, tiles, sub, wide)

    def body(i, _):
        r, tile = i // tiles, i % tiles
        values = widen([raw[r, q * tiles + tile] for q in range(QUARTERS)], width)
        for q in range(QUARTERS):
            east[r, q * tiles + tile] = values[q]
        return 0

    lax.fori_loop(0, rows * tiles, body, 0)


def middle_kernel(width, info, field, from_z, from_c, north, north_z, north_c, east, g, a, h, *refs):
    tables = refs[:10]
    out, edge_z, edge_c, halo, north_halo, ghosts, work, result = refs[10:]
    tiles = field.shape[1] // QUARTERS
    place_halo(info, halo, from_z, from_c)
    place_halo(info, north_halo, north_z, north_c)
    meridional_pass(field, halo, north, north_halo, ghosts, work)
    pole_pass(info, ghosts, work)

    def emit(r, q, tile, value):
        result[r, q * tiles + tile] = value

    zonal_pass(width, work, east, emit)
    solve_pass(result, g, a, h)
    filter_and_edges(result, tables, info, out, edge_z, edge_c)


def last_kernel(width, info, field, from_z, from_c, north, north_z, north_c, east, *refs):
    outs = refs[:4]
    halo, north_halo, ghosts, work, result = refs[4:]
    tiles = field.shape[1] // QUARTERS
    place_halo(info, halo, from_z, from_c)
    place_halo(info, north_halo, north_z, north_c)
    meridional_pass(field, halo, north, north_halo, ghosts, work)
    pole_pass(info, ghosts, work)

    def emit(r, q, tile, value):
        result[r, q * tiles + tile] = value

    zonal_pass(width, work, east, emit)
    for j in range(QUARTERS):
        outs[j][...] = result[:, pl.ds(info[j] * tiles, tiles)]


def call(kernel, outs, scratch, scalars, *args, cost=(1e6, 1e6)):
    shape = lambda s: jax.ShapeDtypeStruct(s, f32)
    specs = [pl.BlockSpec(memory_space=pltpu.SMEM)] * scalars
    specs += [pl.BlockSpec(memory_space=pltpu.VMEM)] * (len(args) - scalars)
    return pl.pallas_call(
        kernel,
        out_shape=[shape(s) for s in outs],
        in_specs=specs,
        out_specs=[pl.BlockSpec(memory_space=pltpu.VMEM)] * len(outs),
        scratch_shapes=[pltpu.VMEM(s, f32) for s in scratch],
        compiler_params=pltpu.CompilerParams(vmem_limit_bytes=48 * 2**20),
        cost_estimate=pl.CostEstimate(flops=int(cost[0]), bytes_accessed=int(cost[1]), transcendentals=0),
    )(*args)


def lat_exchange(edge_z, edge_c):
    count = lax.axis_size("lat")
    pairs = lambda start: [p for i in range(start, count - 1, 2) for p in ((i, i + 1), (i + 1, i))]
    from_z = lax.ppermute(edge_z, "lat", pairs(1))
    from_c = lax.ppermute(edge_c, "lat", pairs(0))
    return from_z, from_c


def on_device(sensitivity, courant_east, courant_north, mixing, cutoff, polar_flag):
    rows, width, channels = sensitivity.shape
    levels = courant_east.shape[2]
    tracers = channels // levels
    tiles = levels // SUB
    parts = lax.axis_size("lon")
    nlon = width * parts
    quarter = nlon // QUARTERS
    wide = round_up(quarter + 2 * HALO, 128)
    me = lax.axis_index("lon")
    lat = lax.axis_index("lat")
    direct = parts == tracers == QUARTERS
    piece = wide if direct else round_up(width, 128)
    tables = fourier_tables(nlon, wide)

    order = jnp.arange(QUARTERS, dtype=jnp.int32)
    if direct:
        order = order ^ me
    ends = jnp.stack([lat % 2, jnp.where(lat == 0, 1, 0), jnp.where(lat == lax.axis_size("lat") - 1, 1, 0), 0 * lat])
    info = jnp.concatenate([order, ends.astype(jnp.int32), cutoff, polar_flag])

    swap = lambda x, s: lax.ppermute(x, "lon", [(i, i ^ s) for i in range(parts)])

    def quarters_of(blocks):
        whole = jnp.moveaxis(blocks[..., :width], 0, -2)
        whole = whole.reshape(whole.shape[:-2] + (QUARTERS, quarter))
        whole = jnp.pad(whole, [(0, 0)] * (whole.ndim - 1) + [(0, wide - quarter)])
        return [whole[..., q, :] for q in range(QUARTERS)]

    def gather(x):
        if direct:
            return [x] + [swap(x, s) for s in range(1, parts)]
        return quarters_of(lax.all_gather(x, "lon"))

    def to_tracers(ys):
        if direct:
            return [ys[0]] + [swap(ys[s], s) for s in range(1, parts)]
        sent = jnp.stack([ys[d % tracers] for d in range(parts)])
        return quarters_of(lax.all_to_all(sent, "lon", split_axis=0, concat_axis=0, tiled=True))

    def to_longitudes(zs):
        if direct:
            return [zs[0]] + [swap(zs[s], s) for s in range(1, parts)]
        whole = jnp.concatenate([z[..., :quarter] for z in zs], axis=-1)
        blocks = jnp.moveaxis(whole.reshape(whole.shape[:-1] + (parts, width)), -2, 0)
        came = lax.all_to_all(blocks, "lon", split_axis=0, concat_axis=0, tiled=True)
        came = jnp.pad(came, [(0, 0)] * (came.ndim - 1) + [(0, piece - width)])
        return [came[t] for t in range(tracers)]

    north_t = courant_north.transpose(0, 2, 1)
    east_t = courant_east.transpose(0, 2, 1)
    mix_t = mixing.transpose(2, 0, 1)
    block = (rows, tiles, SUB, piece)
    full = (rows, QUARTERS * tiles, SUB, wide)
    edge = (HALO,) + full[1:]
    turned = (piece // 128, rows * levels, 128)

    (north_piece,) = call(partial(pack_levels_kernel, tiles), [block], [turned], 0, north_t)
    north_pieces = gather(north_piece)
    ys = call(
        partial(first_solve_kernel, tiles),
        [block] * tracers,
        [(piece // 128, channels, 128), (levels - 1, rows, piece)] + factor_scratch(rows, levels, piece),
        1,
        info,
        sensitivity,
        mix_t,
    )
    pieces = to_tracers(ys)
    (both,) = call(partial(pack_both_kernel, tiles), [(2, rows * tiles, SUB, piece)], [turned], 0, east_t, mix_t)
    both_pieces = gather(both)
    north, north_z, north_c = call(partial(north_kernel, tiles), [full, edge, edge], [], 1, info, *north_pieces)
    north_z, north_c = lat_exchange(north_z, north_c)
    state, edge_z, edge_c = call(
        partial(first_filter_kernel, tiles), [full, edge, edge], [full], 1, info, *pieces, *tables
    )
    edge_z, edge_c = lat_exchange(edge_z, edge_c)
    east, g, a, h = call(
        partial(coefficient_kernel, tiles, quarter),
        [full] * 4,
        [full] + factor_scratch(rows, levels, wide),
        1,
        info,
        *both_pieces,
    )
    halos = [(2 * HALO,) + full[1:]] * 2 + [(4,) + full[1:]] + [full] * 2
    for substep in range(SUBSTEPS - 1):
        state, edge_z, edge_c = call(
            partial(middle_kernel, quarter),
            [full, edge, edge],
            halos,
            1,
            info, state, edge_z, edge_c, north, north_z, north_c, east, g, a, h, *tables,
        )
        edge_z, edge_c = lat_exchange(edge_z, edge_c)
    quarter_block = (rows, tiles, SUB, wide)
    zs = call(
        partial(last_kernel, quarter),
        [quarter_block] * QUARTERS,
        halos,
        1,
        info, state, edge_z, edge_c, north, north_z, north_c, east,
    )
    pieces = to_longitudes(zs)
    (out,) = call(
        partial(unpack_kernel, tiles), [sensitivity.shape], [(piece // 128, channels, 128)], 1, info, *pieces
    )
    return out


def solution(mesh):
    return jax.shard_map(
        on_device,
        mesh=mesh,
        in_specs=(
            P("lat", "lon", None),
            P("lat", "lon", None),
            P("lat", "lon", None),
            P("lat", "lon", None),
            P("lat"),
            P("lat"),
        ),
        out_specs=P("lat", "lon", None),
        check_vma=False,
    )
```

```python
from functools import partial
import math

import jax
import jax.numpy as jnp
import ml_dtypes
import numpy as np
from jax import lax
from jax.experimental import pallas as pl
from jax.experimental.pallas import tpu as pltpu
from jax.sharding import PartitionSpec as P

SUBSTEPS = 2
QUARTERS = 4
HALO = 3
MIDDLE_ROOM = 24
SUB = 8
f32 = jnp.float32
bf16 = jnp.bfloat16


def round_up(n, k):
    return -(-n // k) * k


def fourier_tables(nlon, wide):
    quarter = nlon // 4
    x = np.arange(2 * quarter)
    place = (x // quarter) * wide + x % quarter
    table = np.zeros((2, 2 * wide, round_up(quarter, 128)))
    for odd in (0, 1):
        k = np.arange(odd, quarter, 2)
        n = len(k)
        angle = (x[:, None] * k[None, :] % nlon) * (2.0 * math.pi / nlon)
        table[odd, place, :n] = np.cos(angle)
        table[odd, place, n : 2 * n] = np.sin(angle)
    high = table.astype(np.float32).astype(ml_dtypes.bfloat16)
    low = (table - high.astype(np.float64)).astype(np.float32).astype(ml_dtypes.bfloat16)
    return [high, low]


def wave_index(odd, count, shape):
    n = (count - odd + 1) // 2
    column = lax.broadcasted_iota(jnp.int32, shape, 1)
    wave = 2 * jnp.where(column < n, column, column - n) + odd
    return jnp.where(column < 2 * n, wave, 4 * count)


def split(x):
    high = x.astype(bf16)
    return high, (x - high.astype(f32)).astype(bf16)


def product(high, low, t_high, t_low, side):
    dot = lambda x, t: lax.dot_general(x, t, (((1,), (side,)), ((), ())), preferred_element_type=f32)
    return dot(high, t_high) + dot(low, t_high) + dot(high, t_low)


def column_factors(mix_at, levels, shape, store):
    zero = jnp.zeros(shape, f32)
    h_before = zero
    below = zero
    for level in range(levels):
        above = mix_at(level) if level < levels - 1 else zero
        divisor = 1.0 + below + above - below * h_before
        g = 1.0 / divisor
        h = above * g
        store(level, g, below * g, h)
        h_before = h
        below = above


def column_solve(v, g, a, h):
    n = len(v)
    y = [g[0] * v[0]]
    carry = [a[0]]
    for q in range(1, n):
        y.append(g[q] * v[q] + a[q] * y[q - 1])
        carry.append(a[q] * carry[q - 1])
    z, p = y[n - 1], carry[n - 1]
    step = 1
    while step < SUB:
        z = z + p * pltpu.roll(z, step, 0)
        if 2 * step < SUB:
            p = p * pltpu.roll(p, step, 0)
        step *= 2
    before = pltpu.roll(z, 1, 0)
    y = [y[q] + carry[q] * before for q in range(n - 1)] + [z]
    x = [None] * n
    back = [None] * n
    x[n - 1] = y[n - 1]
    back[n - 1] = h[n - 1]
    for q in range(n - 2, -1, -1):
        x[q] = y[q] + h[q] * x[q + 1]
        back[q] = h[q] * back[q + 1]
    z, p = x[0], back[0]
    step = 1
    while step < SUB:
        z = z + p * pltpu.roll(z, SUB - step, 0)
        if 2 * step < SUB:
            p = p * pltpu.roll(p, SUB - step, 0)
        step *= 2
    after = pltpu.roll(z, SUB - 1, 0)
    return [z] + [x[q] + back[q] * after for q in range(1, n)]


def put(ref, at, value):
    for c in range(ref.shape[0]):
        n = min(128, value.shape[1] - c * 128)
        ref[c, at, :n] = value[:, c * 128 : c * 128 + n]


def get(ref, at):
    return jnp.concatenate([ref[c, at, :] for c in range(ref.shape[0])], axis=1)


def order_of(j, direct):
    return lax.axis_index("lon") ^ j if direct else j


def at_odd():
    return lax.axis_index("lat") % 2


def at_end(end):
    return lax.axis_index("lat") == (lax.axis_size("lat") - 1 if end else 0)


def clear(*refs):
    for ref in refs:
        ref[...] = jnp.zeros(ref.shape, f32)


def factor_scratch(rows, levels, wide):
    return [(wide // 128, rows * levels, 128)] * 3


def first_solve_kernel(tiles, direct, tracers, *refs):
    sens, mix = refs[-(9 + tracers) : -(7 + tracers)]
    outs = refs[-(7 + tracers) : -7]
    turned, g_s, a_s, h_s, sens_v, mix_v, sems = refs[-7:]
    rows, width, channels = sens.shape
    levels = mix.shape[0] + 1
    loads = [pltpu.make_async_copy(mix, mix_v, sems.at[rows])]
    loads += [pltpu.make_async_copy(sens.at[r], sens_v.at[r], sems.at[r]) for r in range(rows)]
    for load in loads:
        load.start()
    clear(turned, g_s, a_s, h_s)
    loads[0].wait()

    def store(level, g, a, h):
        at = pl.ds((level % tiles) * SUB + level // tiles, rows, stride=levels)
        for s, value in ((g_s, g), (a_s, a), (h_s, h)):
            put(s, at, value)

    column_factors(lambda l: mix_v[l], levels, (rows, width), store)
    for r in range(rows):
        loads[r + 1].wait()
        put(turned, slice(0, channels), sens_v[r].T)
        at = lambda q: slice(r * levels + q * SUB, r * levels + q * SUB + SUB)
        g, a, h = ([get(s, at(q)) for q in range(tiles)] for s in (g_s, a_s, h_s))
        for j in range(tracers):
            t = order_of(j, direct)
            v = [get(turned, pl.ds(q * tracers + t, SUB, stride=tiles * tracers)) for q in range(tiles)]
            x = column_solve(v, g, a, h)
            for q in range(tiles):
                outs[j][r, q] = x[q]


def pack_levels_kernel(tiles, *refs):
    src, out, src_v, turned, sems = refs[-5:]
    rows, levels, width = src.shape
    loads = [pltpu.make_async_copy(src.at[r], src_v.at[r], sems.at[r]) for r in range(rows)]
    for load in loads:
        load.start()
    clear(turned)
    for r in range(rows):
        loads[r].wait()
        put(turned, slice(r * levels, (r + 1) * levels), src_v[r])
        for q in range(tiles):
            out[r, q] = get(turned, pl.ds(r * levels + q, SUB, stride=tiles))


def pack_mixing_kernel(*refs):
    mix, out, mix_v, sem = refs[-4:]
    rows, width = mix.shape[1:]
    load = pltpu.make_async_copy(mix, mix_v, sem)
    load.start()
    out[...] = jnp.zeros(out.shape, f32)
    load.wait()
    per = SUB // rows
    for level in range(mix.shape[0]):
        at = level % per * rows
        out[level // per, at : at + rows, :width] = mix_v[level]


def unpack_kernel(tiles, direct, *refs):
    n = len(refs) - 2
    pieces, out, turned = refs[:n], refs[n], refs[n + 1]
    rows, width, channels = out.shape
    for r in range(rows):
        for j in range(n):
            t = order_of(j, direct)
            for q in range(tiles):
                put(turned, pl.ds(q * n + t, SUB, stride=tiles * n), pieces[j][r, q])
        out[r] = get(turned, slice(0, channels))[:, :width].T


def filter_block(count, field, tables, cut, flag, emit):
    rows, groups, sub, wide = field.shape
    tiles = groups // QUARTERS
    levels = tiles * sub
    quarter = [
        field[:, q * tiles : (q + 1) * tiles].reshape(rows * levels, wide) for q in range(QUARTERS)
    ]
    halves = []
    for sign in (0, 1):
        t_high, t_low = (t[sign] for t in tables)
        index = wave_index(sign, count, (levels, t_high.shape[1]))
        scale = jnp.where(index == 0, 1.0, 2.0) / (4 * count)
        if sign:
            pair = [quarter[0] - quarter[2], quarter[1] - quarter[3]]
        else:
            pair = [quarter[0] + quarter[2], quarter[1] + quarter[3]]
        high, low = split(jnp.concatenate(pair, axis=1))
        spectrum = product(high, low, t_high, t_low, 0)
        kept = [
            jnp.where(index <= cut(r), spectrum[r * levels : (r + 1) * levels] * scale, 0.0)
            for r in range(rows)
        ]
        high, low = split(jnp.concatenate(kept, axis=0))
        halves.append(product(high, low, t_high, t_low, 1))
    even, odd = halves
    for r in range(rows):
        at = slice(r * levels, (r + 1) * levels)
        for q in range(QUARTERS):
            lanes = slice((q % 2) * wide, (q % 2 + 1) * wide)
            e, o = even[at, lanes], odd[at, lanes]
            smooth = e + o if q < 2 else e - o
            emit(r, q, jnp.where(flag(r) > 0, smooth, quarter[q][at]))


def load_settings(cutoff, polar_flag, cut_s, flag_s, sems):
    loads = [pltpu.make_async_copy(cutoff, cut_s, sems.at[0]), pltpu.make_async_copy(polar_flag, flag_s, sems.at[1])]
    for load in loads:
        load.start()
    return loads


def settings_scratch(rows):
    return [pltpu.SMEM((rows,), jnp.int32)] * 2 + [pltpu.SemaphoreType.DMA((2,))]


def filter_and_edges(count, field, tables, cutoff, polar_flag, out, edge_z, edge_c):
    rows, groups, sub, wide = field.shape
    tiles = groups // QUARTERS
    active = polar_flag[0]
    for r in range(1, rows):
        active = active | polar_flag[r]

    @pl.when(active > 0)
    def _():
        def emit(r, q, value):
            out[r, q * tiles : (q + 1) * tiles] = value.reshape(tiles, sub, wide)

        filter_block(count, field, tables, lambda r: cutoff[r], lambda r: polar_flag[r], emit)

    @pl.when(active == 0)
    def _():
        out[...] = field[...]

    write_edges(out, edge_z, edge_c)


def write_edges(field, edge_z, edge_c):
    shift = field.shape[0] - HALO
    odd = at_odd()
    edge_z[...] = field[pl.ds(odd * shift, HALO)]
    edge_c[...] = field[pl.ds((1 - odd) * shift, HALO)]


def by_parity(from_z, from_c, body):
    odd = at_odd()

    @pl.when(odd == 1)
    def _():
        body(from_c, from_z)

    @pl.when(odd == 0)
    def _():
        body(from_z, from_c)


def face_weights(courant):
    size = jnp.abs(courant)
    rest = 1.0 - size
    t = courant * rest
    edge = t * rest
    upwind = t * size
    cell = courant * size * (3.0 - 2.0 * size)
    ahead = courant >= 0.0
    small = (1.0 / 12.0) * upwind
    small_plus = jnp.where(ahead, small, 0.0)
    small_minus = small - small_plus
    near = (7.0 / 12.0) * edge
    far = (-1.0 / 12.0) * edge
    large = cell - 7.0 * small
    return {
        -2: small_plus,
        -1: far - 7.0 * small_plus,
        0: near + jnp.where(ahead, large, small),
        1: near + jnp.where(ahead, small, large),
        2: far - 7.0 * small_minus,
        3: small_minus,
    }


def stencil(before, now, m):
    if m == 3:
        return before
    if m == -3:
        return -now
    return before - now + 1.0 if m == 0 else before - now


def north_factors(courant, ghosts, out):
    rows, groups = out.shape[1:3]

    def body(i, _):
        before = None
        for f in range(-HALO, rows + HALO):
            now = face_weights(courant(f, i)) if f < rows + HALO - 1 else None
            for r in range(rows):
                m = f - r
                if -HALO <= m <= HALO:
                    out[m + HALO, r, i] = stencil(
                        before[1 - m] if m > -HALO else None, now[-m] if m < HALO else None, m
                    )
            for end, pole_face, step in ((0, 0, 1), (1, rows - 2, -1)):
                for face, k, slot in ((pole_face, 1, 0), (pole_face + step, 2, 1), (pole_face, 2, 2)):
                    if f == face:

                        @pl.when(at_end(end))
                        def _():
                            ghosts[slot, i] = now[k + 1 if end else -k]

            before = now
        return 0

    lax.fori_loop(0, groups, body, 0)


def meridional_pass(field, before, after, north, out):
    rows, groups, sub, wide = field.shape

    def body(i, _):
        total = [None] * rows
        for g in range(-HALO, rows + HALO):
            if g < 0:
                v = before[g + HALO, i]
            else:
                v = field[g, i] if g < rows else after[g - rows, i]
            for r in range(rows):
                if -HALO <= g - r <= HALO:
                    term = north[g - r + HALO, r, i] * v
                    total[r] = term if total[r] is None else total[r] + term
        for r in range(rows):
            out[r, i] = total[r]
        return 0

    lax.fori_loop(0, groups, body, 0)


def pole_pass(field, ghosts, out):
    rows, groups, sub, wide = out.shape
    half = groups // 2
    for end in (0, 1):

        @pl.when(at_end(end))
        def _():
            first, second, third = (rows - 1, rows - 2, rows - 3) if end else (0, 1, 2)

            def body(i, _):
                j = (i + half) % groups
                v0, v1, v2 = field[first, j], field[second, j], field[third, j]
                near = v0 - v1 if end else v1 - v0
                far = v1 - v2 if end else v2 - v1
                out[first, i] = out[first, i] + ghosts[0, j] * near + ghosts[1, j] * far
                out[second, i] = out[second, i] + ghosts[2, j] * near
                return 0

            lax.fori_loop(0, groups, body, 0)


def widen(values, width):
    wide = values[0].shape[1]
    lane = lax.broadcasted_iota(jnp.int32, values[0].shape, 1)
    result = []
    for q in range(QUARTERS):
        after = pltpu.roll(values[(q + 1) % QUARTERS], width, 1)
        before = pltpu.roll(values[(q - 1) % QUARTERS], wide - width, 1)
        padded = jnp.where(lane < width + HALO, after, before)
        padded = jnp.where((lane >= width + HALO) & (lane < wide - HALO), 0.0, padded)
        result.append(jnp.where(lane < width, values[q], padded))
    return result


def shifted(x, m):
    return x if m == 0 else pltpu.roll(x, -m % x.shape[1], 1)


def zonal_pass(width, field, east, emit):
    rows, groups, sub, wide = field.shape
    tiles = groups // QUARTERS

    def body(i, _):
        r, tile = i // tiles, i % tiles
        values = widen([field[r, q * tiles + tile] for q in range(QUARTERS)], width)
        for q in range(QUARTERS):
            total = None
            for m in range(-HALO, HALO + 1):
                term = east[m + HALO, r, q * tiles + tile] * shifted(values[q], m)
                total = term if total is None else total + term
            emit(r, q, tile, total)
        return 0

    lax.fori_loop(0, rows * tiles, body, 0)


def east_factors(width, courant, out):
    rows, groups, sub, wide = courant.shape
    tiles = groups // QUARTERS

    def body(i, _):
        r, tile = i // tiles, i % tiles
        values = widen([courant[r, q * tiles + tile] for q in range(QUARTERS)], width)
        for q in range(QUARTERS):
            w = {k: shifted(x, -k) for k, x in face_weights(values[q]).items()}
            for m in range(-HALO, HALO + 1):
                out[m + HALO, r, q * tiles + tile] = stencil(w.get(1 - m), w.get(-m), m)
        return 0

    lax.fori_loop(0, rows * tiles, body, 0)


def solve_pass(field, g, a, h):
    rows, groups, sub, wide = field.shape
    tiles = groups // QUARTERS

    def body(i, _):
        r, q = i // QUARTERS, i % QUARTERS
        take = lambda ref: [ref[r, q * tiles + tile] for tile in range(tiles)]
        x = column_solve(take(field), take(g), take(a), take(h))
        for tile in range(tiles):
            field[r, q * tiles + tile] = x[tile]
        return 0

    lax.fori_loop(0, rows * QUARTERS, body, 0)


def place(pieces, tiles, direct, out):
    for j in range(QUARTERS):
        out[:, pl.ds(order_of(j, direct) * tiles, tiles)] = pieces[j][...]


def first_filter_kernel(tiles, direct, count, *refs):
    pieces, tables = refs[:4], refs[4:6]
    cutoff, polar_flag, out, edge_z, edge_c, field, cut_s, flag_s, sems = refs[-9:]
    loads = load_settings(cutoff, polar_flag, cut_s, flag_s, sems)
    place(pieces, tiles, direct, field)
    for load in loads:
        load.wait()
    filter_and_edges(count, field, tables, cut_s, flag_s, out, edge_z, edge_c)


def north_kernel(tiles, direct, *refs):
    pieces = refs[:4]
    out, edge_z, edge_c = refs[-3:]
    place(pieces, tiles, direct, out)

    @pl.when(at_end(1))
    def _():
        out[out.shape[0] - 1] = jnp.zeros(out.shape[1:], f32)

    write_edges(out, edge_z, edge_c)


def north_factor_kernel(north, from_z, from_c, *refs):
    out, ghosts = refs[-2:]
    rows = north.shape[0]

    def body(before, after):
        def courant(g, i):
            if g < 0:
                return before[g + HALO, i]
            return north[g, i] if g < rows else after[g - rows, i]

        north_factors(courant, ghosts, out)

    by_parity(from_z, from_c, body)


def east_factor_kernel(tiles, direct, width, *refs):
    pieces, out, raw = refs[:4], refs[4], refs[5]
    place(pieces, tiles, direct, raw)
    east_factors(width, raw, out)


def column_factor_kernel(tiles, direct, *refs):
    pieces = refs[:4]
    g_o, a_o, h_o, g_s, a_s, h_s = refs[4:]
    rows, groups, sub, wide = g_o.shape
    levels = tiles * sub
    per = SUB // rows
    for j in range(QUARTERS):

        def store(level, g, a, h):
            at = (level % tiles) * SUB + level // tiles
            for s, value in ((g_s, g), (a_s, a), (h_s, h)):
                put(s, pl.ds(at, rows, stride=levels), value)

        mix_at = lambda l: pieces[j][l // per, l % per * rows : l % per * rows + rows, :]
        column_factors(mix_at, levels, (rows, wide), store)
        for s, o in ((g_s, g_o), (a_s, a_o), (h_s, h_o)):
            value = get(s, slice(0, rows * levels)).reshape(rows, tiles, sub, wide)
            o[:, pl.ds(order_of(j, direct) * tiles, tiles)] = value


def advect(width, field, from_z, from_c, north, ghosts, east, work, emit):
    by_parity(from_z, from_c, lambda before, after: meridional_pass(field, before, after, north, work))
    pole_pass(field, ghosts, work)
    zonal_pass(width, work, east, emit)


def middle_kernel(width, field, from_z, from_c, north, ghosts, east, g, a, h, *refs):
    tables = refs[:2]
    cutoff, polar_flag, out, edge_z, edge_c, work, result, cut_s, flag_s, sems = refs[2:]
    loads = load_settings(cutoff, polar_flag, cut_s, flag_s, sems)
    tiles = field.shape[1] // QUARTERS

    def emit(r, q, tile, value):
        result[r, q * tiles + tile] = value

    advect(width, field, from_z, from_c, north, ghosts, east, work, emit)
    solve_pass(result, g, a, h)
    for load in loads:
        load.wait()
    filter_and_edges(width, result, tables, cut_s, flag_s, out, edge_z, edge_c)


def last_kernel(width, direct, field, from_z, from_c, north, ghosts, east, *refs):
    outs = refs[:4]
    work, result = refs[4:]
    tiles = field.shape[1] // QUARTERS

    def emit(r, q, tile, value):
        result[r, q * tiles + tile] = value

    advect(width, field, from_z, from_c, north, ghosts, east, work, emit)
    for j in range(QUARTERS):
        outs[j][...] = result[:, pl.ds(order_of(j, direct) * tiles, tiles)]


def call(kernel, outs, scratch, *args, us=1.0, room=16, outside=()):
    specs = [pl.BlockSpec(memory_space=pltpu.VMEM)] * len(args)
    specs += [pl.BlockSpec(memory_space=pltpu.HBM)] * len(outside)
    return pl.pallas_call(
        kernel,
        out_shape=[jax.ShapeDtypeStruct(s, f32) if isinstance(s, tuple) else s for s in outs],
        in_specs=specs,
        out_specs=[pl.BlockSpec(memory_space=pltpu.VMEM)] * len(outs),
        scratch_shapes=[pltpu.VMEM(s, f32) if isinstance(s, tuple) else s for s in scratch],
        compiler_params=pltpu.CompilerParams(vmem_limit_bytes=room * 2**20),
        cost_estimate=pl.CostEstimate(flops=int(us * 10**9), bytes_accessed=10**5, transcendentals=0),
    )(*args, *outside)


def lat_exchange(edge_z, edge_c):
    count = lax.axis_size("lat")
    pairs = lambda start: [p for i in range(start, count - 1, 2) for p in ((i, i + 1), (i + 1, i))]
    from_z = lax.ppermute(edge_z, "lat", pairs(1))
    from_c = lax.ppermute(edge_c, "lat", pairs(0))
    return from_z, from_c


def on_device(sensitivity, courant_east, courant_north, mixing, cutoff, polar_flag):
    rows, width, channels = sensitivity.shape
    levels = courant_east.shape[2]
    tracers = channels // levels
    tiles = levels // SUB
    parts = lax.axis_size("lon")
    nlon = width * parts
    quarter = nlon // QUARTERS
    wide = round_up(quarter + 2 * HALO, 128)
    direct = parts == tracers == QUARTERS
    piece = wide if direct else round_up(width, 128)
    tables = fourier_tables(nlon, wide)

    swap = lambda x, s: lax.ppermute(x, "lon", [(i, i ^ s) for i in range(parts)])

    def quarters_of(blocks):
        whole = jnp.moveaxis(blocks[..., :width], 0, -2)
        whole = whole.reshape(whole.shape[:-2] + (QUARTERS, quarter))
        whole = jnp.pad(whole, [(0, 0)] * (whole.ndim - 1) + [(0, wide - quarter)])
        return [whole[..., q, :] for q in range(QUARTERS)]

    def gather(x):
        if direct:
            return [x] + [swap(x, s) for s in range(1, parts)]
        return quarters_of(lax.all_gather(x, "lon"))

    def to_tracers(ys):
        if direct:
            return [ys[0]] + [swap(ys[s], s) for s in range(1, parts)]
        sent = jnp.stack([ys[d % tracers] for d in range(parts)])
        return quarters_of(lax.all_to_all(sent, "lon", split_axis=0, concat_axis=0, tiled=True))

    def to_longitudes(zs):
        if direct:
            return [zs[0]] + [swap(zs[s], s) for s in range(1, parts)]
        whole = jnp.concatenate([z[..., :quarter] for z in zs], axis=-1)
        blocks = jnp.moveaxis(whole.reshape(whole.shape[:-1] + (parts, width)), -2, 0)
        came = lax.all_to_all(blocks, "lon", split_axis=0, concat_axis=0, tiled=True)
        came = jnp.pad(came, [(0, 0)] * (came.ndim - 1) + [(0, piece - width)])
        return [came[t] for t in range(tracers)]

    north_t = courant_north.transpose(0, 2, 1)
    east_t = courant_east.transpose(0, 2, 1)
    mix_t = mixing.transpose(2, 0, 1)
    block = (rows, tiles, SUB, piece)
    full = (rows, QUARTERS * tiles, SUB, wide)
    edge = (HALO,) + full[1:]
    turned = (piece // 128, rows * levels, 128)

    def pack(x, *after):
        scratch = [x.shape, turned, pltpu.SemaphoreType.DMA((rows,))]
        return call(partial(pack_levels_kernel, tiles), [block], scratch, *after, outside=[x], us=0.4)[0]

    north_piece = pack(north_t)
    north_pieces = gather(north_piece)
    ys = call(
        partial(first_solve_kernel, tiles, direct, tracers),
        [block] * tracers,
        [(piece // 128, channels, 128)]
        + factor_scratch(rows, levels, piece)
        + [sensitivity.shape, mix_t.shape, pltpu.SemaphoreType.DMA((rows + 1,))],
        north_piece,
        outside=[sensitivity, mix_t],
        us=3.0,
    )
    pieces = to_tracers(ys)
    north, north_z, north_c = call(partial(north_kernel, tiles, direct), [full, edge, edge], [], *north_pieces, ys[0])
    north_z, north_c = lat_exchange(north_z, north_c)
    east_pieces = gather(pack(east_t, *north_pieces[1:]))
    state, edge_z, edge_c = call(
        partial(first_filter_kernel, tiles, direct, quarter),
        [full, edge, edge],
        [full] + settings_scratch(rows),
        *pieces, *tables, north,
        us=2.5,
        outside=[cutoff, polar_flag],
    )
    (mix_piece,) = call(
        pack_mixing_kernel,
        [(rows * tiles, SUB, piece)],
        [mix_t.shape, pltpu.SemaphoreType.DMA(())],
        edge_z,
        outside=[mix_t],
    )
    mix_pieces = gather(mix_piece)
    edges = lat_exchange(edge_z, edge_c)
    north, ghosts = call(
        north_factor_kernel, [(2 * HALO + 1,) + full, (3,) + full[1:]], [], north, north_z, north_c, edge_z
    )
    (east,) = call(
        partial(east_factor_kernel, tiles, direct, quarter), [(2 * HALO + 1,) + full], [full], *east_pieces, us=3.0
    )
    g, a, h = call(
        partial(column_factor_kernel, tiles, direct), [full] * 3, factor_scratch(rows, levels, wide), *mix_pieces, us=2.2
    )
    for substep in range(SUBSTEPS - 1):
        state, edge_z, edge_c = call(
            partial(middle_kernel, quarter),
            [full, edge, edge],
            [full, full] + settings_scratch(rows),
            state, *edges, north, ghosts, east, g, a, h, *tables,
            room=MIDDLE_ROOM,
        us=6.0,
            outside=[cutoff, polar_flag],
        )
        edges = lat_exchange(edge_z, edge_c)
    zs = call(
        partial(last_kernel, quarter, direct),
        [(rows, tiles, SUB, wide)] * QUARTERS,
        [full, full],
        state, *edges, north, ghosts, east,
        us=3.5,
    )
    pieces = to_longitudes(zs)
    (out,) = call(
        partial(unpack_kernel, tiles, direct), [sensitivity.shape], [(piece // 128, channels, 128)], *pieces
    )
    return out


def solution(mesh):
    return jax.shard_map(
        on_device,
        mesh=mesh,
        in_specs=(
            P("lat", "lon", None),
            P("lat", "lon", None),
            P("lat", "lon", None),
            P("lat", "lon", None),
            P("lat"),
            P("lat"),
        ),
        out_specs=P("lat", "lon", None),
        check_vma=False,
    )
```

```python
from functools import partial
import math

import jax
import jax.numpy as jnp
import ml_dtypes
import numpy as np
from jax import lax
from jax.experimental import pallas as pl
from jax.experimental.pallas import tpu as pltpu
from jax.sharding import PartitionSpec as P

SUBSTEPS = 2
QUARTERS = 4
HALO = 3
MIDDLE_ROOM = 16
PACK_US = 0.5
FILTER_US = 2.5
SUB = 8
f32 = jnp.float32
bf16 = jnp.bfloat16


def round_up(n, k):
    return -(-n // k) * k


def fourier_tables(nlon, wide):
    quarter = nlon // 4
    x = np.arange(2 * quarter)
    place = (x // quarter) * wide + x % quarter
    table = np.zeros((2, 2 * wide, round_up(quarter, 128)))
    for odd in (0, 1):
        k = np.arange(odd, quarter, 2)
        n = len(k)
        angle = (x[:, None] * k[None, :] % nlon) * (2.0 * math.pi / nlon)
        table[odd, place, :n] = np.cos(angle)
        table[odd, place, n : 2 * n] = np.sin(angle)
    high = table.astype(np.float32).astype(ml_dtypes.bfloat16)
    low = (table - high.astype(np.float64)).astype(np.float32).astype(ml_dtypes.bfloat16)
    return [high, low]


def wave_index(odd, count, shape):
    n = (count - odd + 1) // 2
    column = lax.broadcasted_iota(jnp.int32, shape, 1)
    wave = 2 * jnp.where(column < n, column, column - n) + odd
    return jnp.where(column < 2 * n, wave, 4 * count)


def split(x):
    high = x.astype(bf16)
    return high, (x - high.astype(f32)).astype(bf16)


def product(high, low, t_high, t_low, side):
    dot = lambda x, t: lax.dot_general(x, t, (((1,), (side,)), ((), ())), preferred_element_type=f32)
    return dot(high, t_high) + dot(low, t_high) + dot(high, t_low)


def column_factors(mix_at, levels, shape, store):
    zero = jnp.zeros(shape, f32)
    h_before = zero
    below = zero
    for level in range(levels):
        above = mix_at(level) if level < levels - 1 else zero
        divisor = 1.0 + below + above - below * h_before
        g = 1.0 / divisor
        h = above * g
        store(level, g, below * g, h)
        h_before = h
        below = above


def column_rest(h):
    n = len(h)
    before = lambda x: [pltpu.roll(x[n - 1], 1, 0)] + x[: n - 1]
    ratio = before(h)
    s = [jnp.ones(h[0].shape, f32)]
    carry = [ratio[0]]
    for q in range(1, n):
        s.append(1.0 + ratio[q] * s[q - 1])
        carry.append(ratio[q] * carry[q - 1])
    z, p = s[n - 1], carry[n - 1]
    step = 1
    while step < SUB:
        z = z + p * pltpu.roll(z, step, 0)
        if 2 * step < SUB:
            p = p * pltpu.roll(p, step, 0)
        step *= 2
    start = pltpu.roll(z, 1, 0)
    s = [s[q] + carry[q] * start for q in range(n - 1)] + [z]
    g = [(1.0 - h[q]) / s[q] for q in range(n)]
    mixing = before([h[q] * s[q] / (1.0 - h[q]) for q in range(n)])
    return g, [mixing[q] * g[q] for q in range(n)]


def column_solve(v, g, a, h):
    n = len(v)
    y = [g[0] * v[0]]
    carry = [a[0]]
    for q in range(1, n):
        y.append(g[q] * v[q] + a[q] * y[q - 1])
        carry.append(a[q] * carry[q - 1])
    z, p = y[n - 1], carry[n - 1]
    step = 1
    while step < SUB:
        z = z + p * pltpu.roll(z, step, 0)
        if 2 * step < SUB:
            p = p * pltpu.roll(p, step, 0)
        step *= 2
    before = pltpu.roll(z, 1, 0)
    y = [y[q] + carry[q] * before for q in range(n - 1)] + [z]
    x = [None] * n
    back = [None] * n
    x[n - 1] = y[n - 1]
    back[n - 1] = h[n - 1]
    for q in range(n - 2, -1, -1):
        x[q] = y[q] + h[q] * x[q + 1]
        back[q] = h[q] * back[q + 1]
    z, p = x[0], back[0]
    step = 1
    while step < SUB:
        z = z + p * pltpu.roll(z, SUB - step, 0)
        if 2 * step < SUB:
            p = p * pltpu.roll(p, SUB - step, 0)
        step *= 2
    after = pltpu.roll(z, SUB - 1, 0)
    return [z] + [x[q] + back[q] * after for q in range(1, n)]


def put(ref, at, value):
    for c in range(ref.shape[0]):
        n = min(128, value.shape[1] - c * 128)
        ref[c, at, :n] = value[:, c * 128 : c * 128 + n]


def get(ref, at):
    return jnp.concatenate([ref[c, at, :] for c in range(ref.shape[0])], axis=1)


def order_of(j, direct):
    return lax.axis_index("lon") ^ j if direct else j


def at_odd():
    return lax.axis_index("lat") % 2


def at_end(end):
    return lax.axis_index("lat") == (lax.axis_size("lat") - 1 if end else 0)


def clear(*refs):
    for ref in refs:
        ref[...] = jnp.zeros(ref.shape, f32)


def factor_scratch(rows, levels, wide):
    return [(wide // 128, rows * levels, 128)] * 3


def first_solve_kernel(tiles, direct, sens, mix, north, *refs):
    rows, width, channels = sens.shape
    levels = mix.shape[0] + 1
    tracers = channels // levels
    outs, h_out = refs[:tracers], refs[tracers]
    turned, packed, g_s, a_s, h_s, sens_v, mix_v, north_v, sems = refs[tracers + 1 :]
    loads = [pltpu.make_async_copy(mix, mix_v, sems.at[2 * rows])]
    loads += [pltpu.make_async_copy(sens.at[r], sens_v.at[r], sems.at[r]) for r in range(rows)]
    loads += [pltpu.make_async_copy(north.at[r], north_v.at[r], sems.at[rows + r]) for r in range(rows)]
    for load in loads:
        load.start()
    clear(turned, packed, g_s, a_s, h_s)
    loads[0].wait()

    def store(level, g, a, h):
        at = pl.ds((level % tiles) * SUB + level // tiles, rows, stride=levels)
        for s, value in ((g_s, g), (a_s, a), (h_s, h)):
            put(s, at, value)

    column_factors(lambda l: mix_v[l], levels, (rows, width), store)
    for r in range(rows):
        loads[1 + r].wait()
        put(turned, slice(0, channels), sens_v[r].T)
        at = lambda q: slice(r * levels + q * SUB, r * levels + q * SUB + SUB)
        g, a, h = ([get(s, at(q)) for q in range(tiles)] for s in (g_s, a_s, h_s))
        for q in range(tiles):
            h_out[r, q] = h[q]
        for j in range(tracers):
            t = order_of(j, direct)
            v = [get(turned, pl.ds(q * tracers + t, SUB, stride=tiles * tracers)) for q in range(tiles)]
            x = column_solve(v, g, a, h)
            for q in range(tiles):
                outs[j][r, q] = x[q]
    for r in range(rows):
        loads[1 + rows + r].wait()
        put(packed, slice(r * levels, (r + 1) * levels), north_v[r])
        for q in range(tiles):
            value = get(packed, pl.ds(r * levels + q, SUB, stride=tiles))
            for j in range(tracers):
                outs[j][rows + r, q] = value


def pack_both_kernel(tiles, h, *refs):
    src, out, src_v, turned, sems = refs[-5:]
    rows, levels, width = src.shape
    loads = [pltpu.make_async_copy(src.at[r], src_v.at[r], sems.at[r]) for r in range(rows)]
    for load in loads:
        load.start()
    clear(turned)
    for r in range(rows):
        for q in range(tiles):
            out[1, r * tiles + q] = h[r, q]
    for r in range(rows):
        loads[r].wait()
        put(turned, slice(r * levels, (r + 1) * levels), src_v[r])
        for q in range(tiles):
            out[0, r * tiles + q] = get(turned, pl.ds(r * levels + q, SUB, stride=tiles))


def unpack_kernel(tiles, direct, *refs):
    n = len(refs) - 2
    pieces, out, turned = refs[:n], refs[n], refs[n + 1]
    rows, width, channels = out.shape
    for r in range(rows):
        for j in range(n):
            t = order_of(j, direct)
            for q in range(tiles):
                put(turned, pl.ds(q * n + t, SUB, stride=tiles * n), pieces[j][r, q])
        out[r] = get(turned, slice(0, channels))[:, :width].T


def filter_block(count, field, tables, cut, flag, emit):
    rows, groups, sub, wide = field.shape
    tiles = groups // QUARTERS
    levels = tiles * sub
    quarter = [
        field[:, q * tiles : (q + 1) * tiles].reshape(rows * levels, wide) for q in range(QUARTERS)
    ]
    halves = []
    for sign in (0, 1):
        t_high, t_low = (t[sign] for t in tables)
        index = wave_index(sign, count, (levels, t_high.shape[1]))
        scale = jnp.where(index == 0, 1.0, 2.0) / (4 * count)
        if sign:
            pair = [quarter[0] - quarter[2], quarter[1] - quarter[3]]
        else:
            pair = [quarter[0] + quarter[2], quarter[1] + quarter[3]]
        high, low = split(jnp.concatenate(pair, axis=1))
        spectrum = product(high, low, t_high, t_low, 0)
        kept = [
            jnp.where(index <= cut(r), spectrum[r * levels : (r + 1) * levels] * scale, 0.0)
            for r in range(rows)
        ]
        high, low = split(jnp.concatenate(kept, axis=0))
        halves.append(product(high, low, t_high, t_low, 1))
    even, odd = halves
    for r in range(rows):
        at = slice(r * levels, (r + 1) * levels)
        for q in range(QUARTERS):
            lanes = slice((q % 2) * wide, (q % 2 + 1) * wide)
            e, o = even[at, lanes], odd[at, lanes]
            smooth = e + o if q < 2 else e - o
            emit(r, q, jnp.where(flag(r) > 0, smooth, quarter[q][at]))


def load_settings(cutoff, polar_flag, cut_s, flag_s, sems):
    loads = [pltpu.make_async_copy(cutoff, cut_s, sems.at[0]), pltpu.make_async_copy(polar_flag, flag_s, sems.at[1])]
    for load in loads:
        load.start()
    return loads


def settings_scratch(rows):
    return [pltpu.SMEM((rows,), jnp.int32)] * 2 + [pltpu.SemaphoreType.DMA((2,))]


def filter_and_edges(count, field, tables, cutoff, polar_flag, out, edge_z, edge_c):
    rows, groups, sub, wide = field.shape
    tiles = groups // QUARTERS
    active = polar_flag[0]
    for r in range(1, rows):
        active = active | polar_flag[r]

    @pl.when(active > 0)
    def _():
        def emit(r, q, value):
            out[r, q * tiles : (q + 1) * tiles] = value.reshape(tiles, sub, wide)

        filter_block(count, field, tables, lambda r: cutoff[r], lambda r: polar_flag[r], emit)

    @pl.when(active == 0)
    def _():
        out[...] = field[...]

    write_edges(out, edge_z, edge_c, 0)


def write_edges(field, edge_z, edge_c, at):
    shift = field.shape[0] - HALO
    odd = at_odd()
    edge_z[at : at + HALO] = field[pl.ds(odd * shift, HALO)]
    edge_c[at : at + HALO] = field[pl.ds((1 - odd) * shift, HALO)]


def by_parity(from_z, from_c, body):
    odd = at_odd()

    @pl.when(odd == 1)
    def _():
        body(from_c, from_z)

    @pl.when(odd == 0)
    def _():
        body(from_z, from_c)


def face_weights(courant):
    size = jnp.abs(courant)
    rest = 1.0 - size
    t = courant * rest
    edge = t * rest
    upwind = t * size
    cell = courant * size * (3.0 - 2.0 * size)
    ahead = courant >= 0.0
    small = (1.0 / 12.0) * upwind
    small_plus = jnp.where(ahead, small, 0.0)
    small_minus = small - small_plus
    near = (7.0 / 12.0) * edge
    far = (-1.0 / 12.0) * edge
    large = cell - 7.0 * small
    return {
        -2: small_plus,
        -1: far - 7.0 * small_plus,
        0: near + jnp.where(ahead, large, small),
        1: near + jnp.where(ahead, small, large),
        2: far - 7.0 * small_minus,
        3: small_minus,
    }


def stencil(before, now, m):
    if m == 3:
        return before
    if m == -3:
        return -now
    return before - now + 1.0 if m == 0 else before - now


def north_factors(courant, ghosts, out):
    rows, groups = out.shape[1:3]

    def body(i, _):
        before = None
        for f in range(-HALO, rows + HALO):
            now = face_weights(courant(f, i)) if f < rows + HALO - 1 else None
            for r in range(rows):
                m = f - r
                if -HALO <= m <= HALO:
                    out[m + HALO, r, i] = stencil(
                        before[1 - m] if m > -HALO else None, now[-m] if m < HALO else None, m
                    )
            for end, pole_face, step in ((0, 0, 1), (1, rows - 2, -1)):
                for face, k, slot in ((pole_face, 1, 0), (pole_face + step, 2, 1), (pole_face, 2, 2)):
                    if f == face:

                        @pl.when(at_end(end))
                        def _():
                            ghosts[slot, i] = now[k + 1 if end else -k]

            before = now
        return 0

    lax.fori_loop(0, groups, body, 0, unroll=2)


def meridional_pass(field, before, after, north, out):
    rows, groups, sub, wide = field.shape

    def body(i, _):
        total = [None] * rows
        for g in range(-HALO, rows + HALO):
            if g < 0:
                v = before[g + HALO, i]
            else:
                v = field[g, i] if g < rows else after[g - rows, i]
            for r in range(rows):
                if -HALO <= g - r <= HALO:
                    term = north[g - r + HALO, r, i] * v
                    total[r] = term if total[r] is None else total[r] + term
        for r in range(rows):
            out[r, i] = total[r]
        return 0

    lax.fori_loop(0, groups, body, 0, unroll=2)


def pole_pass(field, ghosts, out):
    rows, groups, sub, wide = out.shape
    half = groups // 2
    for end in (0, 1):

        @pl.when(at_end(end))
        def _():
            first, second, third = (rows - 1, rows - 2, rows - 3) if end else (0, 1, 2)

            def body(i, _):
                j = (i + half) % groups
                v0, v1, v2 = field[first, j], field[second, j], field[third, j]
                near = v0 - v1 if end else v1 - v0
                far = v1 - v2 if end else v2 - v1
                out[first, i] = out[first, i] + ghosts[0, j] * near + ghosts[1, j] * far
                out[second, i] = out[second, i] + ghosts[2, j] * near
                return 0

            lax.fori_loop(0, groups, body, 0, unroll=2)


def widen(values, width):
    wide = values[0].shape[1]
    lane = lax.broadcasted_iota(jnp.int32, values[0].shape, 1)
    result = []
    for q in range(QUARTERS):
        after = pltpu.roll(values[(q + 1) % QUARTERS], width, 1)
        before = pltpu.roll(values[(q - 1) % QUARTERS], wide - width, 1)
        padded = jnp.where(lane < width + HALO, after, before)
        padded = jnp.where((lane >= width + HALO) & (lane < wide - HALO), 0.0, padded)
        result.append(jnp.where(lane < width, values[q], padded))
    return result


def shifted(x, m):
    return x if m == 0 else pltpu.roll(x, -m % x.shape[1], 1)


def zonal_pass(width, field, east, emit):
    rows, groups, sub, wide = field.shape
    tiles = groups // QUARTERS

    def body(i, _):
        r, tile = i // tiles, i % tiles
        values = widen([field[r, q * tiles + tile] for q in range(QUARTERS)], width)
        for q in range(QUARTERS):
            total = None
            for m in range(-HALO, HALO + 1):
                term = east[m + HALO, r, q * tiles + tile] * shifted(values[q], m)
                total = term if total is None else total + term
            emit(r, q, tile, total)
        return 0

    lax.fori_loop(0, rows * tiles, body, 0, unroll=2)


def east_factors(width, courant, out):
    rows, groups, sub, wide = courant.shape
    tiles = groups // QUARTERS

    def body(i, _):
        r, tile = i // tiles, i % tiles
        values = widen([courant[r, q * tiles + tile] for q in range(QUARTERS)], width)
        for q in range(QUARTERS):
            w = {k: shifted(x, -k) for k, x in face_weights(values[q]).items()}
            for m in range(-HALO, HALO + 1):
                out[m + HALO, r, q * tiles + tile] = stencil(w.get(1 - m), w.get(-m), m)
        return 0

    lax.fori_loop(0, rows * tiles, body, 0, unroll=2)


def solve_pass(field, g, a, h):
    rows, groups, sub, wide = field.shape
    tiles = groups // QUARTERS

    def body(i, _):
        r, q = i // QUARTERS, i % QUARTERS
        take = lambda ref: [ref[r, q * tiles + tile] for tile in range(tiles)]
        x = column_solve(take(field), take(g), take(a), take(h))
        for tile in range(tiles):
            field[r, q * tiles + tile] = x[tile]
        return 0

    lax.fori_loop(0, rows * QUARTERS, body, 0, unroll=2)


def place(pieces, tiles, direct, out):
    for j in range(QUARTERS):
        out[:, pl.ds(order_of(j, direct) * tiles, tiles)] = pieces[j][...]


def first_filter_kernel(tiles, direct, count, *refs):
    pieces, tables = refs[:4], refs[4:6]
    cutoff, polar_flag, out, north, edge_z, edge_c, field, cut_s, flag_s, sems = refs[-10:]
    rows = field.shape[0]
    loads = load_settings(cutoff, polar_flag, cut_s, flag_s, sems)
    for j in range(QUARTERS):
        at = pl.ds(order_of(j, direct) * tiles, tiles)
        field[:, at] = pieces[j][:rows]
        north[:, at] = pieces[j][rows:]

    @pl.when(at_end(1))
    def _():
        north[rows - 1] = jnp.zeros(north.shape[1:], f32)

    write_edges(north, edge_z, edge_c, HALO)
    for load in loads:
        load.wait()
    filter_and_edges(count, field, tables, cut_s, flag_s, out, edge_z, edge_c)


def north_factor_kernel(north, from_z, from_c, *refs):
    out, ghosts = refs[-2:]
    rows = north.shape[0]

    def body(before, after):
        def courant(g, i):
            if g < 0:
                return before[HALO + g + HALO, i]
            return north[g, i] if g < rows else after[HALO + g - rows, i]

        north_factors(courant, ghosts, out)

    by_parity(from_z, from_c, body)


def east_factor_kernel(tiles, direct, width, *refs):
    pieces, out, raw = refs[:4], refs[-2], refs[-1]
    for j in range(QUARTERS):
        at = pl.ds(order_of(j, direct) * tiles, tiles)
        for r in range(raw.shape[0]):
            raw[r, at] = pieces[j][0, r * tiles : (r + 1) * tiles]
    east_factors(width, raw, out)


def column_factor_kernel(tiles, direct, *refs):
    pieces = refs[:4]
    g_o, a_o, h_o = refs[-3:]

    def body(r, _):
        for j in range(QUARTERS):
            h = [pieces[j][1, r * tiles + q] for q in range(tiles)]
            g, a = column_rest(h)
            for q in range(tiles):
                at = order_of(j, direct) * tiles + q
                g_o[r, at] = g[q]
                a_o[r, at] = a[q]
                h_o[r, at] = h[q]
        return 0

    lax.fori_loop(0, g_o.shape[0], body, 0)


def advect(width, field, from_z, from_c, north, ghosts, east, work, emit):
    by_parity(from_z, from_c, lambda before, after: meridional_pass(field, before, after, north, work))
    pole_pass(field, ghosts, work)
    zonal_pass(width, work, east, emit)


def middle_kernel(width, field, from_z, from_c, north, ghosts, east, g, a, h, *refs):
    tables = refs[:2]
    cutoff, polar_flag, out, edge_z, edge_c, work, result, cut_s, flag_s, sems = refs[2:]
    loads = load_settings(cutoff, polar_flag, cut_s, flag_s, sems)
    tiles = field.shape[1] // QUARTERS

    def emit(r, q, tile, value):
        result[r, q * tiles + tile] = value

    advect(width, field, from_z, from_c, north, ghosts, east, work, emit)
    solve_pass(result, g, a, h)
    for load in loads:
        load.wait()
    filter_and_edges(width, result, tables, cut_s, flag_s, out, edge_z, edge_c)


def last_kernel(width, direct, field, from_z, from_c, north, ghosts, east, *refs):
    outs = refs[:4]
    work, result = refs[4:]
    tiles = field.shape[1] // QUARTERS

    def emit(r, q, tile, value):
        result[r, q * tiles + tile] = value

    advect(width, field, from_z, from_c, north, ghosts, east, work, emit)
    for j in range(QUARTERS):
        outs[j][...] = result[:, pl.ds(order_of(j, direct) * tiles, tiles)]


def call(kernel, outs, scratch, *args, us=1.0, room=16, outside=()):
    specs = [pl.BlockSpec(memory_space=pltpu.VMEM)] * len(args)
    specs += [pl.BlockSpec(memory_space=pltpu.HBM)] * len(outside)
    outside = [pltpu.with_memory_space_constraint(x, pltpu.HBM) for x in outside]
    return pl.pallas_call(
        kernel,
        out_shape=[jax.ShapeDtypeStruct(s, f32) if isinstance(s, tuple) else s for s in outs],
        in_specs=specs,
        out_specs=[pl.BlockSpec(memory_space=pltpu.VMEM)] * len(outs),
        scratch_shapes=[pltpu.VMEM(s, f32) if isinstance(s, tuple) else s for s in scratch],
        compiler_params=pltpu.CompilerParams(vmem_limit_bytes=room * 2**20),
        cost_estimate=pl.CostEstimate(flops=int(us * 10**9), bytes_accessed=10**5, transcendentals=0),
    )(*args, *outside)


def lat_exchange(edge_z, edge_c):
    count = lax.axis_size("lat")
    pairs = lambda start: [p for i in range(start, count - 1, 2) for p in ((i, i + 1), (i + 1, i))]
    from_z = lax.ppermute(edge_z, "lat", pairs(1))
    from_c = lax.ppermute(edge_c, "lat", pairs(0))
    return from_z, from_c


def on_device(sensitivity, courant_east, courant_north, mixing, cutoff, polar_flag):
    rows, width, channels = sensitivity.shape
    levels = courant_east.shape[2]
    tracers = channels // levels
    tiles = levels // SUB
    parts = lax.axis_size("lon")
    nlon = width * parts
    quarter = nlon // QUARTERS
    wide = round_up(quarter + 2 * HALO, 128)
    direct = parts == tracers == QUARTERS
    piece = wide if direct else round_up(width, 128)
    tables = fourier_tables(nlon, wide)

    swap = lambda x, s: lax.ppermute(x, "lon", [(i, i ^ s) for i in range(parts)])

    def quarters_of(blocks):
        whole = jnp.moveaxis(blocks[..., :width], 0, -2)
        whole = whole.reshape(whole.shape[:-2] + (QUARTERS, quarter))
        whole = jnp.pad(whole, [(0, 0)] * (whole.ndim - 1) + [(0, wide - quarter)])
        return [whole[..., q, :] for q in range(QUARTERS)]

    def gather(x):
        if direct:
            return [x] + [swap(x, s) for s in range(1, parts)]
        return quarters_of(lax.all_gather(x, "lon"))

    def to_tracers(ys):
        if direct:
            return [ys[0]] + [swap(ys[s], s) for s in range(1, parts)]
        sent = jnp.stack([ys[d % tracers] for d in range(parts)])
        return quarters_of(lax.all_to_all(sent, "lon", split_axis=0, concat_axis=0, tiled=True))

    def to_longitudes(zs):
        if direct:
            return [zs[0]] + [swap(zs[s], s) for s in range(1, parts)]
        whole = jnp.concatenate([z[..., :quarter] for z in zs], axis=-1)
        blocks = jnp.moveaxis(whole.reshape(whole.shape[:-1] + (parts, width)), -2, 0)
        came = lax.all_to_all(blocks, "lon", split_axis=0, concat_axis=0, tiled=True)
        came = jnp.pad(came, [(0, 0)] * (came.ndim - 1) + [(0, piece - width)])
        return [came[t] for t in range(tracers)]

    north_t = courant_north.transpose(0, 2, 1)
    east_t = courant_east.transpose(0, 2, 1)
    mix_t = mixing.transpose(2, 0, 1)
    block = (rows, tiles, SUB, piece)
    full = (rows, QUARTERS * tiles, SUB, wide)
    edge = (HALO,) + full[1:]
    turned = (piece // 128, rows * levels, 128)

    *ys, h_piece = call(
        partial(first_solve_kernel, tiles, direct),
        [(2 * rows,) + block[1:]] * tracers + [block],
        [(piece // 128, channels, 128), turned]
        + factor_scratch(rows, levels, piece)
        + [sensitivity.shape, mix_t.shape, north_t.shape, pltpu.SemaphoreType.DMA((2 * rows + 1,))],
        outside=[sensitivity, mix_t, north_t],
        us=3.0,
    )
    pieces = to_tracers(ys)
    (both,) = call(
        partial(pack_both_kernel, tiles),
        [(2, rows * tiles, SUB, piece)],
        [east_t.shape, turned, pltpu.SemaphoreType.DMA((rows,))],
        h_piece, *pieces[1:],
        outside=[east_t],
        us=PACK_US,
    )
    both_pieces = gather(both)
    both_edge = (2 * HALO,) + full[1:]
    state, north, edge_z, edge_c = call(
        partial(first_filter_kernel, tiles, direct, quarter),
        [full, full, both_edge, both_edge],
        [full] + settings_scratch(rows),
        *pieces, *tables, both,
        us=FILTER_US,
        outside=[cutoff, polar_flag],
    )
    edges = lat_exchange(edge_z, edge_c)
    (east,) = call(
        partial(east_factor_kernel, tiles, direct, quarter), [(2 * HALO + 1,) + full], [full], *both_pieces, us=10.0
    )
    g, a, h = call(
        partial(column_factor_kernel, tiles, direct),
        [full] * 3,
        [],
        *both_pieces,
        us=10.0,
    )
    north, ghosts = call(
        north_factor_kernel, [(2 * HALO + 1,) + full, (3,) + full[1:]], [], north, *edges, us=1.5
    )
    for substep in range(SUBSTEPS - 1):
        state, edge_z, edge_c = call(
            partial(middle_kernel, quarter),
            [full, edge, edge],
            [full, full] + settings_scratch(rows),
            state, *edges, north, ghosts, east, g, a, h, *tables,
            room=MIDDLE_ROOM,
        us=6.0,
            outside=[cutoff, polar_flag],
        )
        edges = lat_exchange(edge_z, edge_c)
    zs = call(
        partial(last_kernel, quarter, direct),
        [(rows, tiles, SUB, wide)] * QUARTERS,
        [full, full],
        state, *edges, north, ghosts, east,
        us=3.5,
    )
    pieces = to_longitudes(zs)
    (out,) = call(
        partial(unpack_kernel, tiles, direct), [sensitivity.shape], [(piece // 128, channels, 128)], *pieces
    )
    return out


def solution(mesh):
    return jax.shard_map(
        on_device,
        mesh=mesh,
        in_specs=(
            P("lat", "lon", None),
            P("lat", "lon", None),
            P("lat", "lon", None),
            P("lat", "lon", None),
            P("lat"),
            P("lat"),
        ),
        out_specs=P("lat", "lon", None),
        check_vma=False,
    )
```

```python
from functools import partial
import math

import jax
import jax.numpy as jnp
import ml_dtypes
import numpy as np
from jax import lax
from jax.experimental import pallas as pl
from jax.experimental.pallas import tpu as pltpu
from jax.sharding import PartitionSpec as P

SUBSTEPS = 2
QUARTERS = 4
HALO = 3
MIDDLE_ROOM = 16
PACK_US = 0.5
FILTER_US = 2.5
SUB = 8
f32 = jnp.float32
bf16 = jnp.bfloat16


def round_up(n, k):
    return -(-n // k) * k


def fourier_tables(nlon, wide):
    quarter = nlon // 4
    x = np.arange(2 * quarter)
    place = (x // quarter) * wide + x % quarter
    table = np.zeros((2, 2 * wide, round_up(quarter, 128)))
    for odd in (0, 1):
        k = np.arange(odd, quarter, 2)
        n = len(k)
        angle = (x[:, None] * k[None, :] % nlon) * (2.0 * math.pi / nlon)
        table[odd, place, :n] = np.cos(angle)
        table[odd, place, n : 2 * n] = np.sin(angle)
    high = table.astype(np.float32).astype(ml_dtypes.bfloat16)
    low = (table - high.astype(np.float64)).astype(np.float32).astype(ml_dtypes.bfloat16)
    return [high, low]


def wave_index(odd, count, shape):
    n = (count - odd + 1) // 2
    column = lax.broadcasted_iota(jnp.int32, shape, 1)
    wave = 2 * jnp.where(column < n, column, column - n) + odd
    return jnp.where(column < 2 * n, wave, 4 * count)


def split(x):
    high = x.astype(bf16)
    return high, (x - high.astype(f32)).astype(bf16)


def product(high, low, t_high, t_low, side):
    dot = lambda x, t: lax.dot_general(x, t, (((1,), (side,)), ((), ())), preferred_element_type=f32)
    return dot(high, t_high) + dot(low, t_high) + dot(high, t_low)


def column_factors(mix_at, levels, shape, store):
    zero = jnp.zeros(shape, f32)
    h_before = zero
    below = zero
    for level in range(levels):
        above = mix_at(level) if level < levels - 1 else zero
        divisor = 1.0 + below + above - below * h_before
        g = 1.0 / divisor
        h = above * g
        store(level, g, below * g, h)
        h_before = h
        below = above


def column_rest(h):
    n = len(h)
    before = lambda x: [pltpu.roll(x[n - 1], 1, 0)] + x[: n - 1]
    ratio = before(h)
    s = [jnp.ones(h[0].shape, f32)]
    carry = [ratio[0]]
    for q in range(1, n):
        s.append(1.0 + ratio[q] * s[q - 1])
        carry.append(ratio[q] * carry[q - 1])
    z, p = s[n - 1], carry[n - 1]
    step = 1
    while step < SUB:
        z = z + p * pltpu.roll(z, step, 0)
        if 2 * step < SUB:
            p = p * pltpu.roll(p, step, 0)
        step *= 2
    start = pltpu.roll(z, 1, 0)
    s = [s[q] + carry[q] * start for q in range(n - 1)] + [z]
    g = [(1.0 - h[q]) / s[q] for q in range(n)]
    mixing = before([h[q] * s[q] / (1.0 - h[q]) for q in range(n)])
    return g, [mixing[q] * g[q] for q in range(n)]


def column_solve(v, g, a, h):
    n = len(v)
    y = [g[0] * v[0]]
    carry = [a[0]]
    for q in range(1, n):
        y.append(g[q] * v[q] + a[q] * y[q - 1])
        carry.append(a[q] * carry[q - 1])
    z, p = y[n - 1], carry[n - 1]
    step = 1
    while step < SUB:
        z = z + p * pltpu.roll(z, step, 0)
        if 2 * step < SUB:
            p = p * pltpu.roll(p, step, 0)
        step *= 2
    before = pltpu.roll(z, 1, 0)
    y = [y[q] + carry[q] * before for q in range(n - 1)] + [z]
    x = [None] * n
    back = [None] * n
    x[n - 1] = y[n - 1]
    back[n - 1] = h[n - 1]
    for q in range(n - 2, -1, -1):
        x[q] = y[q] + h[q] * x[q + 1]
        back[q] = h[q] * back[q + 1]
    z, p = x[0], back[0]
    step = 1
    while step < SUB:
        z = z + p * pltpu.roll(z, SUB - step, 0)
        if 2 * step < SUB:
            p = p * pltpu.roll(p, SUB - step, 0)
        step *= 2
    after = pltpu.roll(z, SUB - 1, 0)
    return [z] + [x[q] + back[q] * after for q in range(1, n)]


def put(ref, at, value):
    for c in range(ref.shape[0]):
        n = min(128, value.shape[1] - c * 128)
        ref[c, at, :n] = value[:, c * 128 : c * 128 + n]


def get(ref, at):
    return jnp.concatenate([ref[c, at, :] for c in range(ref.shape[0])], axis=1)


def order_of(j, direct):
    return lax.axis_index("lon") ^ j if direct else j


def at_odd():
    return lax.axis_index("lat") % 2


def at_end(end):
    return lax.axis_index("lat") == (lax.axis_size("lat") - 1 if end else 0)


def clear(*refs):
    for ref in refs:
        ref[...] = jnp.zeros(ref.shape, f32)


def factor_scratch(rows, levels, wide):
    return [(wide // 128, rows * levels, 128)] * 3


def first_solve_kernel(tiles, direct, sens, mix, north, *refs):
    rows, width, channels = sens.shape
    levels = mix.shape[0] + 1
    tracers = channels // levels
    outs, h_out = refs[:tracers], refs[tracers]
    turned, packed, g_s, a_s, h_s, sens_v, mix_v, north_v, sems = refs[tracers + 1 :]
    loads = [pltpu.make_async_copy(mix, mix_v, sems.at[2 * rows])]
    loads += [pltpu.make_async_copy(sens.at[r], sens_v.at[r], sems.at[r]) for r in range(rows)]
    loads += [pltpu.make_async_copy(north.at[r], north_v.at[r], sems.at[rows + r]) for r in range(rows)]
    for load in loads:
        load.start()
    clear(turned, packed, g_s, a_s, h_s)
    loads[0].wait()

    def store(level, g, a, h):
        at = pl.ds((level % tiles) * SUB + level // tiles, rows, stride=levels)
        for s, value in ((g_s, g), (a_s, a), (h_s, h)):
            put(s, at, value)

    column_factors(lambda l: mix_v[l], levels, (rows, width), store)
    for r in range(rows):
        loads[1 + r].wait()
        put(turned, slice(0, channels), sens_v[r].T)
        at = lambda q: slice(r * levels + q * SUB, r * levels + q * SUB + SUB)
        g, a, h = ([get(s, at(q)) for q in range(tiles)] for s in (g_s, a_s, h_s))
        for q in range(tiles):
            h_out[r, q] = h[q]
        for j in range(tracers):
            t = order_of(j, direct)
            v = [get(turned, pl.ds(q * tracers + t, SUB, stride=tiles * tracers)) for q in range(tiles)]
            x = column_solve(v, g, a, h)
            for q in range(tiles):
                outs[j][r, q] = x[q]
    for r in range(rows):
        loads[1 + rows + r].wait()
        put(packed, slice(r * levels, (r + 1) * levels), north_v[r])
        for q in range(tiles):
            value = get(packed, pl.ds(r * levels + q, SUB, stride=tiles))
            for j in range(tracers):
                outs[j][rows + r, q] = value


def pack_both_kernel(tiles, h, *refs):
    src, out, src_v, turned, sems = refs[-5:]
    rows, levels, width = src.shape
    loads = [pltpu.make_async_copy(src.at[r], src_v.at[r], sems.at[r]) for r in range(rows)]
    for load in loads:
        load.start()
    clear(turned)
    for r in range(rows):
        for q in range(tiles):
            out[1, r * tiles + q] = h[r, q]
    for r in range(rows):
        loads[r].wait()
        put(turned, slice(r * levels, (r + 1) * levels), src_v[r])
        for q in range(tiles):
            out[0, r * tiles + q] = get(turned, pl.ds(r * levels + q, SUB, stride=tiles))


def unpack_kernel(tiles, direct, *refs):
    n = len(refs) - 2
    pieces, out, turned = refs[:n], refs[n], refs[n + 1]
    rows, width, channels = out.shape
    for r in range(rows):
        for j in range(n):
            t = order_of(j, direct)
            for q in range(tiles):
                put(turned, pl.ds(q * n + t, SUB, stride=tiles * n), pieces[j][r, q])
        out[r] = get(turned, slice(0, channels))[:, :width].T


def filter_block(count, field, tables, cut, flag, emit):
    rows, groups, sub, wide = field.shape
    tiles = groups // QUARTERS
    levels = tiles * sub
    quarter = [
        field[:, q * tiles : (q + 1) * tiles].reshape(rows * levels, wide) for q in range(QUARTERS)
    ]
    halves = []
    for sign in (0, 1):
        t_high, t_low = (t[sign] for t in tables)
        index = wave_index(sign, count, (levels, t_high.shape[1]))
        scale = jnp.where(index == 0, 1.0, 2.0) / (4 * count)
        if sign:
            pair = [quarter[0] - quarter[2], quarter[1] - quarter[3]]
        else:
            pair = [quarter[0] + quarter[2], quarter[1] + quarter[3]]
        high, low = split(jnp.concatenate(pair, axis=1))
        spectrum = product(high, low, t_high, t_low, 0)
        kept = [
            jnp.where(index <= cut(r), spectrum[r * levels : (r + 1) * levels] * scale, 0.0)
            for r in range(rows)
        ]
        high, low = split(jnp.concatenate(kept, axis=0))
        halves.append(product(high, low, t_high, t_low, 1))
    even, odd = halves
    for r in range(rows):
        at = slice(r * levels, (r + 1) * levels)
        for q in range(QUARTERS):
            lanes = slice((q % 2) * wide, (q % 2 + 1) * wide)
            e, o = even[at, lanes], odd[at, lanes]
            smooth = e + o if q < 2 else e - o
            emit(r, q, jnp.where(flag(r) > 0, smooth, quarter[q][at]))


def load_settings(cutoff, polar_flag, cut_s, flag_s, sems):
    loads = [pltpu.make_async_copy(cutoff, cut_s, sems.at[0]), pltpu.make_async_copy(polar_flag, flag_s, sems.at[1])]
    for load in loads:
        load.start()
    return loads


def settings_scratch(rows):
    return [pltpu.SMEM((rows,), jnp.int32)] * 2 + [pltpu.SemaphoreType.DMA((2,))]


def filter_and_edges(count, field, tables, cutoff, polar_flag, out, edge_z, edge_c):
    rows, groups, sub, wide = field.shape
    tiles = groups // QUARTERS
    active = polar_flag[0]
    for r in range(1, rows):
        active = active | polar_flag[r]

    @pl.when(active > 0)
    def _():
        def emit(r, q, value):
            out[r, q * tiles : (q + 1) * tiles] = value.reshape(tiles, sub, wide)

        filter_block(count, field, tables, lambda r: cutoff[r], lambda r: polar_flag[r], emit)

    @pl.when(active == 0)
    def _():
        out[...] = field[...]

    write_edges(out, edge_z, edge_c, 0)


def write_edges(field, edge_z, edge_c, at):
    shift = field.shape[0] - HALO
    odd = at_odd()
    edge_z[at : at + HALO] = field[pl.ds(odd * shift, HALO)]
    edge_c[at : at + HALO] = field[pl.ds((1 - odd) * shift, HALO)]


def by_parity(from_z, from_c, body):
    odd = at_odd()

    @pl.when(odd == 1)
    def _():
        body(from_c, from_z)

    @pl.when(odd == 0)
    def _():
        body(from_z, from_c)


def face_weights(courant):
    size = jnp.abs(courant)
    rest = 1.0 - size
    t = courant * rest
    edge = t * rest
    upwind = t * size
    cell = courant * size * (3.0 - 2.0 * size)
    ahead = courant >= 0.0
    small = (1.0 / 12.0) * upwind
    small_plus = jnp.where(ahead, small, 0.0)
    small_minus = small - small_plus
    near = (7.0 / 12.0) * edge
    far = (-1.0 / 12.0) * edge
    large = cell - 7.0 * small
    return {
        -2: small_plus,
        -1: far - 7.0 * small_plus,
        0: near + jnp.where(ahead, large, small),
        1: near + jnp.where(ahead, small, large),
        2: far - 7.0 * small_minus,
        3: small_minus,
    }


def stencil(before, now, m):
    if m == 3:
        return before
    if m == -3:
        return -now
    return before - now + 1.0 if m == 0 else before - now


def north_factors(courant, ghosts, out):
    rows, groups = out.shape[1:3]

    def body(i, _):
        before = None
        for f in range(-HALO, rows + HALO):
            now = face_weights(courant(f, i)) if f < rows + HALO - 1 else None
            for r in range(rows):
                m = f - r
                if -HALO <= m <= HALO:
                    out[m + HALO, r, i] = stencil(
                        before[1 - m] if m > -HALO else None, now[-m] if m < HALO else None, m
                    )
            for end, pole_face, step in ((0, 0, 1), (1, rows - 2, -1)):
                for face, k, slot in ((pole_face, 1, 0), (pole_face + step, 2, 1), (pole_face, 2, 2)):
                    if f == face:

                        @pl.when(at_end(end))
                        def _():
                            ghosts[slot, i] = now[k + 1 if end else -k]

            before = now
        return 0

    lax.fori_loop(0, groups, body, 0, unroll=4)


def meridional_pass(field, before, after, north, out):
    rows, groups, sub, wide = field.shape

    def body(i, _):
        total = [None] * rows
        for g in range(-HALO, rows + HALO):
            if g < 0:
                v = before[g + HALO, i]
            else:
                v = field[g, i] if g < rows else after[g - rows, i]
            for r in range(rows):
                if -HALO <= g - r <= HALO:
                    term = north[g - r + HALO, r, i] * v
                    total[r] = term if total[r] is None else total[r] + term
        for r in range(rows):
            out[r, i] = total[r]
        return 0

    lax.fori_loop(0, groups, body, 0, unroll=4)


def pole_pass(field, ghosts, out):
    rows, groups, sub, wide = out.shape
    half = groups // 2
    for end in (0, 1):

        @pl.when(at_end(end))
        def _():
            first, second, third = (rows - 1, rows - 2, rows - 3) if end else (0, 1, 2)

            def body(i, _):
                j = (i + half) % groups
                v0, v1, v2 = field[first, j], field[second, j], field[third, j]
                near = v0 - v1 if end else v1 - v0
                far = v1 - v2 if end else v2 - v1
                out[first, i] = out[first, i] + ghosts[0, j] * near + ghosts[1, j] * far
                out[second, i] = out[second, i] + ghosts[2, j] * near
                return 0

            lax.fori_loop(0, groups, body, 0, unroll=4)


def widen(values, width):
    wide = values[0].shape[1]
    lane = lax.broadcasted_iota(jnp.int32, values[0].shape, 1)
    result = []
    for q in range(QUARTERS):
        after = pltpu.roll(values[(q + 1) % QUARTERS], width, 1)
        before = pltpu.roll(values[(q - 1) % QUARTERS], wide - width, 1)
        padded = jnp.where(lane < width + HALO, after, before)
        padded = jnp.where((lane >= width + HALO) & (lane < wide - HALO), 0.0, padded)
        result.append(jnp.where(lane < width, values[q], padded))
    return result


def shifted(x, m):
    return x if m == 0 else pltpu.roll(x, -m % x.shape[1], 1)


def zonal_pass(width, field, east, emit):
    rows, groups, sub, wide = field.shape
    tiles = groups // QUARTERS

    def body(i, _):
        r, tile = i // tiles, i % tiles
        values = widen([field[r, q * tiles + tile] for q in range(QUARTERS)], width)
        for q in range(QUARTERS):
            total = None
            for m in range(-HALO, HALO + 1):
                term = east[m + HALO, r, q * tiles + tile] * shifted(values[q], m)
                total = term if total is None else total + term
            emit(r, q, tile, total)
        return 0

    lax.fori_loop(0, rows * tiles, body, 0, unroll=4)


def east_factors(width, courant, out):
    rows, groups, sub, wide = courant.shape
    tiles = groups // QUARTERS

    def body(i, _):
        r, tile = i // tiles, i % tiles
        values = widen([courant[r, q * tiles + tile] for q in range(QUARTERS)], width)
        for q in range(QUARTERS):
            w = {k: shifted(x, -k) for k, x in face_weights(values[q]).items()}
            for m in range(-HALO, HALO + 1):
                out[m + HALO, r, q * tiles + tile] = stencil(w.get(1 - m), w.get(-m), m)
        return 0

    lax.fori_loop(0, rows * tiles, body, 0, unroll=4)


def solve_pass(field, g, a, h):
    rows, groups, sub, wide = field.shape
    tiles = groups // QUARTERS

    def body(i, _):
        r, q = i // QUARTERS, i % QUARTERS
        take = lambda ref: [ref[r, q * tiles + tile] for tile in range(tiles)]
        x = column_solve(take(field), take(g), take(a), take(h))
        for tile in range(tiles):
            field[r, q * tiles + tile] = x[tile]
        return 0

    lax.fori_loop(0, rows * QUARTERS, body, 0, unroll=4)


def place(pieces, tiles, direct, out):
    for j in range(QUARTERS):
        out[:, pl.ds(order_of(j, direct) * tiles, tiles)] = pieces[j][...]


def first_filter_kernel(tiles, direct, count, *refs):
    pieces, tables = refs[:4], refs[4:6]
    cutoff, polar_flag, out, north, edge_z, edge_c, field, cut_s, flag_s, sems = refs[-10:]
    rows = field.shape[0]
    loads = load_settings(cutoff, polar_flag, cut_s, flag_s, sems)
    for j in range(QUARTERS):
        at = pl.ds(order_of(j, direct) * tiles, tiles)
        field[:, at] = pieces[j][:rows]
        north[:, at] = pieces[j][rows:]

    @pl.when(at_end(1))
    def _():
        north[rows - 1] = jnp.zeros(north.shape[1:], f32)

    write_edges(north, edge_z, edge_c, HALO)
    for load in loads:
        load.wait()
    filter_and_edges(count, field, tables, cut_s, flag_s, out, edge_z, edge_c)


def north_factor_kernel(north, from_z, from_c, *refs):
    out, ghosts = refs[-2:]
    rows = north.shape[0]

    def body(before, after):
        def courant(g, i):
            if g < 0:
                return before[HALO + g + HALO, i]
            return north[g, i] if g < rows else after[HALO + g - rows, i]

        north_factors(courant, ghosts, out)

    by_parity(from_z, from_c, body)


def east_factor_kernel(tiles, direct, width, *refs):
    pieces, out, raw = refs[:4], refs[-2], refs[-1]
    for j in range(QUARTERS):
        at = pl.ds(order_of(j, direct) * tiles, tiles)
        for r in range(raw.shape[0]):
            raw[r, at] = pieces[j][0, r * tiles : (r + 1) * tiles]
    east_factors(width, raw, out)


def column_factor_kernel(tiles, direct, *refs):
    pieces = refs[:4]
    g_o, a_o, h_o = refs[-3:]

    def body(r, _):
        for j in range(QUARTERS):
            h = [pieces[j][1, r * tiles + q] for q in range(tiles)]
            g, a = column_rest(h)
            for q in range(tiles):
                at = order_of(j, direct) * tiles + q
                g_o[r, at] = g[q]
                a_o[r, at] = a[q]
                h_o[r, at] = h[q]
        return 0

    lax.fori_loop(0, g_o.shape[0], body, 0)


def advect(width, field, from_z, from_c, north, ghosts, east, work, emit):
    by_parity(from_z, from_c, lambda before, after: meridional_pass(field, before, after, north, work))
    pole_pass(field, ghosts, work)
    zonal_pass(width, work, east, emit)


def middle_kernel(width, field, from_z, from_c, north, ghosts, east, g, a, h, *refs):
    tables = refs[:2]
    cutoff, polar_flag, out, edge_z, edge_c, work, result, cut_s, flag_s, sems = refs[2:]
    loads = load_settings(cutoff, polar_flag, cut_s, flag_s, sems)
    tiles = field.shape[1] // QUARTERS

    def emit(r, q, tile, value):
        result[r, q * tiles + tile] = value

    advect(width, field, from_z, from_c, north, ghosts, east, work, emit)
    solve_pass(result, g, a, h)
    for load in loads:
        load.wait()
    filter_and_edges(width, result, tables, cut_s, flag_s, out, edge_z, edge_c)


def last_kernel(width, direct, field, from_z, from_c, north, ghosts, east, *refs):
    outs = refs[:4]
    work, result = refs[4:]
    tiles = field.shape[1] // QUARTERS

    def emit(r, q, tile, value):
        result[r, q * tiles + tile] = value

    advect(width, field, from_z, from_c, north, ghosts, east, work, emit)
    for j in range(QUARTERS):
        outs[j][...] = result[:, pl.ds(order_of(j, direct) * tiles, tiles)]


def call(kernel, outs, scratch, *args, us=1.0, room=16, outside=()):
    specs = [pl.BlockSpec(memory_space=pltpu.VMEM)] * len(args)
    specs += [pl.BlockSpec(memory_space=pltpu.HBM)] * len(outside)
    outside = [pltpu.with_memory_space_constraint(x, pltpu.HBM) for x in outside]
    return pl.pallas_call(
        kernel,
        out_shape=[jax.ShapeDtypeStruct(s, f32) if isinstance(s, tuple) else s for s in outs],
        in_specs=specs,
        out_specs=[pl.BlockSpec(memory_space=pltpu.VMEM)] * len(outs),
        scratch_shapes=[pltpu.VMEM(s, f32) if isinstance(s, tuple) else s for s in scratch],
        compiler_params=pltpu.CompilerParams(vmem_limit_bytes=room * 2**20),
        cost_estimate=pl.CostEstimate(flops=int(us * 10**9), bytes_accessed=10**5, transcendentals=0),
    )(*args, *outside)


def lat_exchange(edge_z, edge_c):
    count = lax.axis_size("lat")
    pairs = lambda start: [p for i in range(start, count - 1, 2) for p in ((i, i + 1), (i + 1, i))]
    from_z = lax.ppermute(edge_z, "lat", pairs(1))
    from_c = lax.ppermute(edge_c, "lat", pairs(0))
    return from_z, from_c


def on_device(sensitivity, courant_east, courant_north, mixing, cutoff, polar_flag):
    rows, width, channels = sensitivity.shape
    levels = courant_east.shape[2]
    tracers = channels // levels
    tiles = levels // SUB
    parts = lax.axis_size("lon")
    nlon = width * parts
    quarter = nlon // QUARTERS
    wide = round_up(quarter + 2 * HALO, 128)
    direct = parts == tracers == QUARTERS
    piece = wide if direct else round_up(width, 128)
    tables = fourier_tables(nlon, wide)

    swap = lambda x, s: lax.ppermute(x, "lon", [(i, i ^ s) for i in range(parts)])

    def quarters_of(blocks):
        whole = jnp.moveaxis(blocks[..., :width], 0, -2)
        whole = whole.reshape(whole.shape[:-2] + (QUARTERS, quarter))
        whole = jnp.pad(whole, [(0, 0)] * (whole.ndim - 1) + [(0, wide - quarter)])
        return [whole[..., q, :] for q in range(QUARTERS)]

    def gather(x):
        if direct:
            return [x] + [swap(x, s) for s in range(1, parts)]
        return quarters_of(lax.all_gather(x, "lon"))

    def to_tracers(ys):
        if direct:
            return [ys[0]] + [swap(ys[s], s) for s in range(1, parts)]
        sent = jnp.stack([ys[d % tracers] for d in range(parts)])
        return quarters_of(lax.all_to_all(sent, "lon", split_axis=0, concat_axis=0, tiled=True))

    def to_longitudes(zs):
        if direct:
            return [zs[0]] + [swap(zs[s], s) for s in range(1, parts)]
        whole = jnp.concatenate([z[..., :quarter] for z in zs], axis=-1)
        blocks = jnp.moveaxis(whole.reshape(whole.shape[:-1] + (parts, width)), -2, 0)
        came = lax.all_to_all(blocks, "lon", split_axis=0, concat_axis=0, tiled=True)
        came = jnp.pad(came, [(0, 0)] * (came.ndim - 1) + [(0, piece - width)])
        return [came[t] for t in range(tracers)]

    north_t = courant_north.transpose(0, 2, 1)
    east_t = courant_east.transpose(0, 2, 1)
    mix_t = mixing.transpose(2, 0, 1)
    block = (rows, tiles, SUB, piece)
    full = (rows, QUARTERS * tiles, SUB, wide)
    edge = (HALO,) + full[1:]
    turned = (piece // 128, rows * levels, 128)

    *ys, h_piece = call(
        partial(first_solve_kernel, tiles, direct),
        [(2 * rows,) + block[1:]] * tracers + [block],
        [(piece // 128, channels, 128), turned]
        + factor_scratch(rows, levels, piece)
        + [sensitivity.shape, mix_t.shape, north_t.shape, pltpu.SemaphoreType.DMA((2 * rows + 1,))],
        outside=[sensitivity, mix_t, north_t],
        us=3.0,
    )
    pieces = to_tracers(ys)
    (both,) = call(
        partial(pack_both_kernel, tiles),
        [(2, rows * tiles, SUB, piece)],
        [east_t.shape, turned, pltpu.SemaphoreType.DMA((rows,))],
        h_piece, *pieces[1:],
        outside=[east_t],
        us=PACK_US,
    )
    both_pieces = gather(both)
    both_edge = (2 * HALO,) + full[1:]
    state, north, edge_z, edge_c = call(
        partial(first_filter_kernel, tiles, direct, quarter),
        [full, full, both_edge, both_edge],
        [full] + settings_scratch(rows),
        *pieces, *tables, both,
        us=FILTER_US,
        outside=[cutoff, polar_flag],
    )
    edges = lat_exchange(edge_z, edge_c)
    (east,) = call(
        partial(east_factor_kernel, tiles, direct, quarter), [(2 * HALO + 1,) + full], [full], *both_pieces, us=10.0
    )
    g, a, h = call(
        partial(column_factor_kernel, tiles, direct),
        [full] * 3,
        [],
        *both_pieces,
        us=10.0,
    )
    north, ghosts = call(
        north_factor_kernel, [(2 * HALO + 1,) + full, (3,) + full[1:]], [], north, *edges, us=1.5
    )
    for substep in range(SUBSTEPS - 1):
        state, edge_z, edge_c = call(
            partial(middle_kernel, quarter),
            [full, edge, edge],
            [full, full] + settings_scratch(rows),
            state, *edges, north, ghosts, east, g, a, h, *tables,
            room=MIDDLE_ROOM,
        us=6.0,
            outside=[cutoff, polar_flag],
        )
        edges = lat_exchange(edge_z, edge_c)
    zs = call(
        partial(last_kernel, quarter, direct),
        [(rows, tiles, SUB, wide)] * QUARTERS,
        [full, full],
        state, *edges, north, ghosts, east,
        us=3.5,
    )
    pieces = to_longitudes(zs)
    (out,) = call(
        partial(unpack_kernel, tiles, direct), [sensitivity.shape], [(piece // 128, channels, 128)], *pieces
    )
    return out


def solution(mesh):
    return jax.shard_map(
        on_device,
        mesh=mesh,
        in_specs=(
            P("lat", "lon", None),
            P("lat", "lon", None),
            P("lat", "lon", None),
            P("lat", "lon", None),
            P("lat"),
            P("lat"),
        ),
        out_specs=P("lat", "lon", None),
        check_vma=False,
    )
```

```python
from functools import partial
import math

import jax
import jax.numpy as jnp
import ml_dtypes
import numpy as np
from jax import lax
from jax.experimental import pallas as pl
from jax.experimental.pallas import tpu as pltpu
from jax.sharding import PartitionSpec as P

SUBSTEPS = 2
QUARTERS = 4
HALO = 3
MIDDLE_ROOM = 16
PACK_US = 0.5
FILTER_US = 2.5
SUB = 8
f32 = jnp.float32
bf16 = jnp.bfloat16


def round_up(n, k):
    return -(-n // k) * k


def fourier_tables(nlon, wide):
    quarter = nlon // 4
    x = np.arange(2 * quarter)
    place = (x // quarter) * wide + x % quarter
    table = np.zeros((2, 2 * wide, round_up(quarter, 128)))
    for odd in (0, 1):
        k = np.arange(odd, quarter, 2)
        n = len(k)
        angle = (x[:, None] * k[None, :] % nlon) * (2.0 * math.pi / nlon)
        table[odd, place, :n] = np.cos(angle)
        table[odd, place, n : 2 * n] = np.sin(angle)
    high = table.astype(np.float32).astype(ml_dtypes.bfloat16)
    low = (table - high.astype(np.float64)).astype(np.float32).astype(ml_dtypes.bfloat16)
    return [high, low]


def wave_index(odd, count, shape):
    n = (count - odd + 1) // 2
    column = lax.broadcasted_iota(jnp.int32, shape, 1)
    wave = 2 * jnp.where(column < n, column, column - n) + odd
    return jnp.where(column < 2 * n, wave, 4 * count)


def split(x):
    high = x.astype(bf16)
    return high, (x - high.astype(f32)).astype(bf16)


def product(high, low, t_high, t_low, side):
    dot = lambda x, t: lax.dot_general(x, t, (((1,), (side,)), ((), ())), preferred_element_type=f32)
    n = high.shape[0]
    both = dot(jnp.concatenate([high, low], axis=0), t_high)
    return both[:n] + both[n:] + dot(high, t_low)


def column_factors(mix_at, levels, shape, store):
    zero = jnp.zeros(shape, f32)
    h_before = zero
    below = zero
    for level in range(levels):
        above = mix_at(level) if level < levels - 1 else zero
        divisor = 1.0 + below + above - below * h_before
        g = 1.0 / divisor
        h = above * g
        store(level, g, below * g, h)
        h_before = h
        below = above


def column_rest(h):
    n = len(h)
    before = lambda x: [pltpu.roll(x[n - 1], 1, 0)] + x[: n - 1]
    ratio = before(h)
    s = [jnp.ones(h[0].shape, f32)]
    carry = [ratio[0]]
    for q in range(1, n):
        s.append(1.0 + ratio[q] * s[q - 1])
        carry.append(ratio[q] * carry[q - 1])
    z, p = s[n - 1], carry[n - 1]
    step = 1
    while step < SUB:
        z = z + p * pltpu.roll(z, step, 0)
        if 2 * step < SUB:
            p = p * pltpu.roll(p, step, 0)
        step *= 2
    start = pltpu.roll(z, 1, 0)
    s = [s[q] + carry[q] * start for q in range(n - 1)] + [z]
    g = [(1.0 - h[q]) / s[q] for q in range(n)]
    mixing = before([h[q] * s[q] / (1.0 - h[q]) for q in range(n)])
    return g, [mixing[q] * g[q] for q in range(n)]


def column_solve(v, g, a, h):
    n = len(v)
    y = [g[0] * v[0]]
    carry = [a[0]]
    for q in range(1, n):
        y.append(g[q] * v[q] + a[q] * y[q - 1])
        carry.append(a[q] * carry[q - 1])
    z, p = y[n - 1], carry[n - 1]
    step = 1
    while step < SUB:
        z = z + p * pltpu.roll(z, step, 0)
        if 2 * step < SUB:
            p = p * pltpu.roll(p, step, 0)
        step *= 2
    before = pltpu.roll(z, 1, 0)
    y = [y[q] + carry[q] * before for q in range(n - 1)] + [z]
    x = [None] * n
    back = [None] * n
    x[n - 1] = y[n - 1]
    back[n - 1] = h[n - 1]
    for q in range(n - 2, -1, -1):
        x[q] = y[q] + h[q] * x[q + 1]
        back[q] = h[q] * back[q + 1]
    z, p = x[0], back[0]
    step = 1
    while step < SUB:
        z = z + p * pltpu.roll(z, SUB - step, 0)
        if 2 * step < SUB:
            p = p * pltpu.roll(p, SUB - step, 0)
        step *= 2
    after = pltpu.roll(z, SUB - 1, 0)
    return [z] + [x[q] + back[q] * after for q in range(1, n)]


def put(ref, at, value):
    for c in range(ref.shape[0]):
        n = min(128, value.shape[1] - c * 128)
        ref[c, at, :n] = value[:, c * 128 : c * 128 + n]


def get(ref, at):
    return jnp.concatenate([ref[c, at, :] for c in range(ref.shape[0])], axis=1)


def order_of(j, direct):
    return lax.axis_index("lon") ^ j if direct else j


def at_odd():
    return lax.axis_index("lat") % 2


def at_end(end):
    return lax.axis_index("lat") == (lax.axis_size("lat") - 1 if end else 0)


def clear(*refs):
    for ref in refs:
        ref[...] = jnp.zeros(ref.shape, f32)


def factor_scratch(rows, levels, wide):
    return [(wide // 128, rows * levels, 128)] * 3


def first_solve_kernel(tiles, direct, sens, mix, north, *refs):
    rows, width, channels = sens.shape
    levels = mix.shape[0] + 1
    tracers = channels // levels
    outs, h_out = refs[:tracers], refs[tracers]
    turned, packed, g_s, a_s, h_s, sens_v, mix_v, north_v, sems = refs[tracers + 1 :]
    loads = [pltpu.make_async_copy(mix, mix_v, sems.at[2 * rows])]
    loads += [pltpu.make_async_copy(sens.at[r], sens_v.at[r], sems.at[r]) for r in range(rows)]
    loads += [pltpu.make_async_copy(north.at[r], north_v.at[r], sems.at[rows + r]) for r in range(rows)]
    for load in loads:
        load.start()
    clear(turned, packed, g_s, a_s, h_s)
    loads[0].wait()

    def store(level, g, a, h):
        at = pl.ds((level % tiles) * SUB + level // tiles, rows, stride=levels)
        for s, value in ((g_s, g), (a_s, a), (h_s, h)):
            put(s, at, value)

    column_factors(lambda l: mix_v[l], levels, (rows, width), store)
    for r in range(rows):
        loads[1 + r].wait()
        put(turned, slice(0, channels), sens_v[r].T)
        at = lambda q: slice(r * levels + q * SUB, r * levels + q * SUB + SUB)
        g, a, h = ([get(s, at(q)) for q in range(tiles)] for s in (g_s, a_s, h_s))
        for q in range(tiles):
            h_out[r, q] = h[q]
        for j in range(tracers):
            t = order_of(j, direct)
            v = [get(turned, pl.ds(q * tracers + t, SUB, stride=tiles * tracers)) for q in range(tiles)]
            x = column_solve(v, g, a, h)
            for q in range(tiles):
                outs[j][r, q] = x[q]
    for r in range(rows):
        loads[1 + rows + r].wait()
        put(packed, slice(r * levels, (r + 1) * levels), north_v[r])
        for q in range(tiles):
            value = get(packed, pl.ds(r * levels + q, SUB, stride=tiles))
            for j in range(tracers):
                outs[j][rows + r, q] = value


def pack_both_kernel(tiles, h, *refs):
    src, out, src_v, turned, sems = refs[-5:]
    rows, levels, width = src.shape
    loads = [pltpu.make_async_copy(src.at[r], src_v.at[r], sems.at[r]) for r in range(rows)]
    for load in loads:
        load.start()
    clear(turned)
    for r in range(rows):
        for q in range(tiles):
            out[1, r * tiles + q] = h[r, q]
    for r in range(rows):
        loads[r].wait()
        put(turned, slice(r * levels, (r + 1) * levels), src_v[r])
        for q in range(tiles):
            out[0, r * tiles + q] = get(turned, pl.ds(r * levels + q, SUB, stride=tiles))


def unpack_kernel(tiles, direct, *refs):
    n = len(refs) - 2
    pieces, out, turned = refs[:n], refs[n], refs[n + 1]
    rows, width, channels = out.shape
    for r in range(rows):
        for j in range(n):
            t = order_of(j, direct)
            for q in range(tiles):
                put(turned, pl.ds(q * n + t, SUB, stride=tiles * n), pieces[j][r, q])
        out[r] = get(turned, slice(0, channels))[:, :width].T


def filter_block(count, field, tables, cut, flag, emit):
    rows, groups, sub, wide = field.shape
    tiles = groups // QUARTERS
    levels = tiles * sub
    quarter = [
        field[:, q * tiles : (q + 1) * tiles].reshape(rows * levels, wide) for q in range(QUARTERS)
    ]
    halves = []
    for sign in (0, 1):
        t_high, t_low = (t[sign] for t in tables)
        index = wave_index(sign, count, (levels, t_high.shape[1]))
        scale = jnp.where(index == 0, 1.0, 2.0) / (4 * count)
        if sign:
            pair = [quarter[0] - quarter[2], quarter[1] - quarter[3]]
        else:
            pair = [quarter[0] + quarter[2], quarter[1] + quarter[3]]
        high, low = split(jnp.concatenate(pair, axis=1))
        spectrum = product(high, low, t_high, t_low, 0)
        kept = [
            jnp.where(index <= cut(r), spectrum[r * levels : (r + 1) * levels] * scale, 0.0)
            for r in range(rows)
        ]
        high, low = split(jnp.concatenate(kept, axis=0))
        halves.append(product(high, low, t_high, t_low, 1))
    even, odd = halves
    for r in range(rows):
        at = slice(r * levels, (r + 1) * levels)
        for q in range(QUARTERS):
            lanes = slice((q % 2) * wide, (q % 2 + 1) * wide)
            e, o = even[at, lanes], odd[at, lanes]
            smooth = e + o if q < 2 else e - o
            emit(r, q, jnp.where(flag(r) > 0, smooth, quarter[q][at]))


def load_settings(cutoff, polar_flag, cut_s, flag_s, sems):
    loads = [pltpu.make_async_copy(cutoff, cut_s, sems.at[0]), pltpu.make_async_copy(polar_flag, flag_s, sems.at[1])]
    for load in loads:
        load.start()
    return loads


def settings_scratch(rows):
    return [pltpu.SMEM((rows,), jnp.int32)] * 2 + [pltpu.SemaphoreType.DMA((2,))]


def filter_and_edges(count, field, tables, cutoff, polar_flag, out, edge_z, edge_c):
    rows, groups, sub, wide = field.shape
    tiles = groups // QUARTERS
    active = polar_flag[0]
    for r in range(1, rows):
        active = active | polar_flag[r]

    @pl.when(active > 0)
    def _():
        def emit(r, q, value):
            out[r, q * tiles : (q + 1) * tiles] = value.reshape(tiles, sub, wide)

        filter_block(count, field, tables, lambda r: cutoff[r], lambda r: polar_flag[r], emit)

    @pl.when(active == 0)
    def _():
        out[...] = field[...]

    write_edges(out, edge_z, edge_c, 0)


def write_edges(field, edge_z, edge_c, at):
    shift = field.shape[0] - HALO
    odd = at_odd()
    edge_z[at : at + HALO] = field[pl.ds(odd * shift, HALO)]
    edge_c[at : at + HALO] = field[pl.ds((1 - odd) * shift, HALO)]


def by_parity(from_z, from_c, body):
    odd = at_odd()

    @pl.when(odd == 1)
    def _():
        body(from_c, from_z)

    @pl.when(odd == 0)
    def _():
        body(from_z, from_c)


def face_weights(courant):
    size = jnp.abs(courant)
    rest = 1.0 - size
    t = courant * rest
    edge = t * rest
    upwind = t * size
    cell = courant * size * (3.0 - 2.0 * size)
    ahead = courant >= 0.0
    small = (1.0 / 12.0) * upwind
    small_plus = jnp.where(ahead, small, 0.0)
    small_minus = small - small_plus
    near = (7.0 / 12.0) * edge
    far = (-1.0 / 12.0) * edge
    large = cell - 7.0 * small
    return {
        -2: small_plus,
        -1: far - 7.0 * small_plus,
        0: near + jnp.where(ahead, large, small),
        1: near + jnp.where(ahead, small, large),
        2: far - 7.0 * small_minus,
        3: small_minus,
    }


def stencil(before, now, m):
    if m == 3:
        return before
    if m == -3:
        return -now
    return before - now + 1.0 if m == 0 else before - now


def north_factors(courant, ghosts, out):
    rows, groups = out.shape[1:3]

    def body(i, _):
        before = None
        for f in range(-HALO, rows + HALO):
            now = face_weights(courant(f, i)) if f < rows + HALO - 1 else None
            for r in range(rows):
                m = f - r
                if -HALO <= m <= HALO:
                    out[m + HALO, r, i] = stencil(
                        before[1 - m] if m > -HALO else None, now[-m] if m < HALO else None, m
                    )
            for end, pole_face, step in ((0, 0, 1), (1, rows - 2, -1)):
                for face, k, slot in ((pole_face, 1, 0), (pole_face + step, 2, 1), (pole_face, 2, 2)):
                    if f == face:

                        @pl.when(at_end(end))
                        def _():
                            ghosts[slot, i] = now[k + 1 if end else -k]

            before = now
        return 0

    lax.fori_loop(0, groups, body, 0, unroll=4)


def meridional_pass(field, before, after, north, out):
    rows, groups, sub, wide = field.shape

    def body(i, _):
        total = [None] * rows
        for g in range(-HALO, rows + HALO):
            if g < 0:
                v = before[g + HALO, i]
            else:
                v = field[g, i] if g < rows else after[g - rows, i]
            for r in range(rows):
                if -HALO <= g - r <= HALO:
                    term = north[g - r + HALO, r, i] * v
                    total[r] = term if total[r] is None else total[r] + term
        for r in range(rows):
            out[r, i] = total[r]
        return 0

    lax.fori_loop(0, groups, body, 0, unroll=4)


def pole_pass(field, ghosts, out):
    rows, groups, sub, wide = out.shape
    half = groups // 2
    for end in (0, 1):

        @pl.when(at_end(end))
        def _():
            first, second, third = (rows - 1, rows - 2, rows - 3) if end else (0, 1, 2)

            def body(i, _):
                j = (i + half) % groups
                v0, v1, v2 = field[first, j], field[second, j], field[third, j]
                near = v0 - v1 if end else v1 - v0
                far = v1 - v2 if end else v2 - v1
                out[first, i] = out[first, i] + ghosts[0, j] * near + ghosts[1, j] * far
                out[second, i] = out[second, i] + ghosts[2, j] * near
                return 0

            lax.fori_loop(0, groups, body, 0, unroll=4)


def widen(values, width):
    wide = values[0].shape[1]
    lane = lax.broadcasted_iota(jnp.int32, values[0].shape, 1)
    result = []
    for q in range(QUARTERS):
        after = pltpu.roll(values[(q + 1) % QUARTERS], width, 1)
        before = pltpu.roll(values[(q - 1) % QUARTERS], wide - width, 1)
        padded = jnp.where(lane < width + HALO, after, before)
        padded = jnp.where((lane >= width + HALO) & (lane < wide - HALO), 0.0, padded)
        result.append(jnp.where(lane < width, values[q], padded))
    return result


def shifted(x, m):
    return x if m == 0 else pltpu.roll(x, -m % x.shape[1], 1)


def zonal_pass(width, field, east, emit):
    rows, groups, sub, wide = field.shape
    tiles = groups // QUARTERS

    def body(i, _):
        r, tile = i // tiles, i % tiles
        values = widen([field[r, q * tiles + tile] for q in range(QUARTERS)], width)
        for q in range(QUARTERS):
            total = None
            for m in range(-HALO, HALO + 1):
                term = east[m + HALO, r, q * tiles + tile] * shifted(values[q], m)
                total = term if total is None else total + term
            emit(r, q, tile, total)
        return 0

    lax.fori_loop(0, rows * tiles, body, 0, unroll=4)


def east_factors(width, courant, out):
    rows, groups, sub, wide = courant.shape
    tiles = groups // QUARTERS

    def body(i, _):
        r, tile = i // tiles, i % tiles
        values = widen([courant[r, q * tiles + tile] for q in range(QUARTERS)], width)
        for q in range(QUARTERS):
            w = {k: shifted(x, -k) for k, x in face_weights(values[q]).items()}
            for m in range(-HALO, HALO + 1):
                out[m + HALO, r, q * tiles + tile] = stencil(w.get(1 - m), w.get(-m), m)
        return 0

    lax.fori_loop(0, rows * tiles, body, 0, unroll=4)


def solve_pass(field, g, a, h):
    rows, groups, sub, wide = field.shape
    tiles = groups // QUARTERS

    def body(i, _):
        r, q = i // QUARTERS, i % QUARTERS
        take = lambda ref: [ref[r, q * tiles + tile] for tile in range(tiles)]
        x = column_solve(take(field), take(g), take(a), take(h))
        for tile in range(tiles):
            field[r, q * tiles + tile] = x[tile]
        return 0

    lax.fori_loop(0, rows * QUARTERS, body, 0, unroll=4)


def place(pieces, tiles, direct, out):
    for j in range(QUARTERS):
        out[:, pl.ds(order_of(j, direct) * tiles, tiles)] = pieces[j][...]


def first_filter_kernel(tiles, direct, count, *refs):
    pieces, tables = refs[:4], refs[4:6]
    cutoff, polar_flag, out, north, edge_z, edge_c, field, cut_s, flag_s, sems = refs[-10:]
    rows = field.shape[0]
    loads = load_settings(cutoff, polar_flag, cut_s, flag_s, sems)
    for j in range(QUARTERS):
        at = pl.ds(order_of(j, direct) * tiles, tiles)
        field[:, at] = pieces[j][:rows]
        north[:, at] = pieces[j][rows:]

    @pl.when(at_end(1))
    def _():
        north[rows - 1] = jnp.zeros(north.shape[1:], f32)

    write_edges(north, edge_z, edge_c, HALO)
    for load in loads:
        load.wait()
    filter_and_edges(count, field, tables, cut_s, flag_s, out, edge_z, edge_c)


def north_factor_kernel(north, from_z, from_c, *refs):
    out, ghosts = refs[-2:]
    rows = north.shape[0]

    def body(before, after):
        def courant(g, i):
            if g < 0:
                return before[HALO + g + HALO, i]
            return north[g, i] if g < rows else after[HALO + g - rows, i]

        north_factors(courant, ghosts, out)

    by_parity(from_z, from_c, body)


def east_factor_kernel(tiles, direct, width, *refs):
    pieces, out, raw = refs[:4], refs[-2], refs[-1]
    for j in range(QUARTERS):
        at = pl.ds(order_of(j, direct) * tiles, tiles)
        for r in range(raw.shape[0]):
            raw[r, at] = pieces[j][0, r * tiles : (r + 1) * tiles]
    east_factors(width, raw, out)


def column_factor_kernel(tiles, direct, *refs):
    pieces = refs[:4]
    g_o, a_o, h_o = refs[-3:]

    def body(r, _):
        for j in range(QUARTERS):
            h = [pieces[j][1, r * tiles + q] for q in range(tiles)]
            g, a = column_rest(h)
            for q in range(tiles):
                at = order_of(j, direct) * tiles + q
                g_o[r, at] = g[q]
                a_o[r, at] = a[q]
                h_o[r, at] = h[q]
        return 0

    lax.fori_loop(0, g_o.shape[0], body, 0)


def advect(width, field, from_z, from_c, north, ghosts, east, work, emit):
    by_parity(from_z, from_c, lambda before, after: meridional_pass(field, before, after, north, work))
    pole_pass(field, ghosts, work)
    zonal_pass(width, work, east, emit)


def middle_kernel(width, field, from_z, from_c, north, ghosts, east, g, a, h, *refs):
    tables = refs[:2]
    cutoff, polar_flag, out, edge_z, edge_c, work, result, cut_s, flag_s, sems = refs[2:]
    loads = load_settings(cutoff, polar_flag, cut_s, flag_s, sems)
    tiles = field.shape[1] // QUARTERS

    def emit(r, q, tile, value):
        result[r, q * tiles + tile] = value

    advect(width, field, from_z, from_c, north, ghosts, east, work, emit)
    solve_pass(result, g, a, h)
    for load in loads:
        load.wait()
    filter_and_edges(width, result, tables, cut_s, flag_s, out, edge_z, edge_c)


def last_kernel(width, direct, field, from_z, from_c, north, ghosts, east, *refs):
    outs = refs[:4]
    work, result = refs[4:]
    tiles = field.shape[1] // QUARTERS

    def emit(r, q, tile, value):
        result[r, q * tiles + tile] = value

    advect(width, field, from_z, from_c, north, ghosts, east, work, emit)
    for j in range(QUARTERS):
        outs[j][...] = result[:, pl.ds(order_of(j, direct) * tiles, tiles)]


def call(kernel, outs, scratch, *args, us=1.0, room=16, outside=()):
    specs = [pl.BlockSpec(memory_space=pltpu.VMEM)] * len(args)
    specs += [pl.BlockSpec(memory_space=pltpu.HBM)] * len(outside)
    outside = [pltpu.with_memory_space_constraint(x, pltpu.HBM) for x in outside]
    return pl.pallas_call(
        kernel,
        out_shape=[jax.ShapeDtypeStruct(s, f32) if isinstance(s, tuple) else s for s in outs],
        in_specs=specs,
        out_specs=[pl.BlockSpec(memory_space=pltpu.VMEM)] * len(outs),
        scratch_shapes=[pltpu.VMEM(s, f32) if isinstance(s, tuple) else s for s in scratch],
        compiler_params=pltpu.CompilerParams(vmem_limit_bytes=room * 2**20),
        cost_estimate=pl.CostEstimate(flops=int(us * 10**9), bytes_accessed=10**5, transcendentals=0),
    )(*args, *outside)


def lat_exchange(edge_z, edge_c):
    count = lax.axis_size("lat")
    pairs = lambda start: [p for i in range(start, count - 1, 2) for p in ((i, i + 1), (i + 1, i))]
    from_z = lax.ppermute(edge_z, "lat", pairs(1))
    from_c = lax.ppermute(edge_c, "lat", pairs(0))
    return from_z, from_c


def on_device(sensitivity, courant_east, courant_north, mixing, cutoff, polar_flag):
    rows, width, channels = sensitivity.shape
    levels = courant_east.shape[2]
    tracers = channels // levels
    tiles = levels // SUB
    parts = lax.axis_size("lon")
    nlon = width * parts
    quarter = nlon // QUARTERS
    wide = round_up(quarter + 2 * HALO, 128)
    direct = parts == tracers == QUARTERS
    piece = wide if direct else round_up(width, 128)
    tables = fourier_tables(nlon, wide)

    swap = lambda x, s: lax.ppermute(x, "lon", [(i, i ^ s) for i in range(parts)])

    def quarters_of(blocks):
        whole = jnp.moveaxis(blocks[..., :width], 0, -2)
        whole = whole.reshape(whole.shape[:-2] + (QUARTERS, quarter))
        whole = jnp.pad(whole, [(0, 0)] * (whole.ndim - 1) + [(0, wide - quarter)])
        return [whole[..., q, :] for q in range(QUARTERS)]

    def gather(x):
        if direct:
            return [x] + [swap(x, s) for s in range(1, parts)]
        return quarters_of(lax.all_gather(x, "lon"))

    def to_tracers(ys):
        if direct:
            return [ys[0]] + [swap(ys[s], s) for s in range(1, parts)]
        sent = jnp.stack([ys[d % tracers] for d in range(parts)])
        return quarters_of(lax.all_to_all(sent, "lon", split_axis=0, concat_axis=0, tiled=True))

    def to_longitudes(zs):
        if direct:
            return [zs[0]] + [swap(zs[s], s) for s in range(1, parts)]
        whole = jnp.concatenate([z[..., :quarter] for z in zs], axis=-1)
        blocks = jnp.moveaxis(whole.reshape(whole.shape[:-1] + (parts, width)), -2, 0)
        came = lax.all_to_all(blocks, "lon", split_axis=0, concat_axis=0, tiled=True)
        came = jnp.pad(came, [(0, 0)] * (came.ndim - 1) + [(0, piece - width)])
        return [came[t] for t in range(tracers)]

    north_t = courant_north.transpose(0, 2, 1)
    east_t = courant_east.transpose(0, 2, 1)
    mix_t = mixing.transpose(2, 0, 1)
    block = (rows, tiles, SUB, piece)
    full = (rows, QUARTERS * tiles, SUB, wide)
    edge = (HALO,) + full[1:]
    turned = (piece // 128, rows * levels, 128)

    *ys, h_piece = call(
        partial(first_solve_kernel, tiles, direct),
        [(2 * rows,) + block[1:]] * tracers + [block],
        [(piece // 128, channels, 128), turned]
        + factor_scratch(rows, levels, piece)
        + [sensitivity.shape, mix_t.shape, north_t.shape, pltpu.SemaphoreType.DMA((2 * rows + 1,))],
        outside=[sensitivity, mix_t, north_t],
        us=3.0,
    )
    pieces = to_tracers(ys)
    (both,) = call(
        partial(pack_both_kernel, tiles),
        [(2, rows * tiles, SUB, piece)],
        [east_t.shape, turned, pltpu.SemaphoreType.DMA((rows,))],
        h_piece, *pieces[1:],
        outside=[east_t],
        us=PACK_US,
    )
    both_pieces = gather(both)
    both_edge = (2 * HALO,) + full[1:]
    state, north, edge_z, edge_c = call(
        partial(first_filter_kernel, tiles, direct, quarter),
        [full, full, both_edge, both_edge],
        [full] + settings_scratch(rows),
        *pieces, *tables, both,
        us=FILTER_US,
        outside=[cutoff, polar_flag],
    )
    edges = lat_exchange(edge_z, edge_c)
    (east,) = call(
        partial(east_factor_kernel, tiles, direct, quarter), [(2 * HALO + 1,) + full], [full], *both_pieces, us=10.0
    )
    g, a, h = call(
        partial(column_factor_kernel, tiles, direct),
        [full] * 3,
        [],
        *both_pieces,
        us=10.0,
    )
    north, ghosts = call(
        north_factor_kernel, [(2 * HALO + 1,) + full, (3,) + full[1:]], [], north, *edges, us=1.5
    )
    for substep in range(SUBSTEPS - 1):
        state, edge_z, edge_c = call(
            partial(middle_kernel, quarter),
            [full, edge, edge],
            [full, full] + settings_scratch(rows),
            state, *edges, north, ghosts, east, g, a, h, *tables,
            room=MIDDLE_ROOM,
        us=6.0,
            outside=[cutoff, polar_flag],
        )
        edges = lat_exchange(edge_z, edge_c)
    zs = call(
        partial(last_kernel, quarter, direct),
        [(rows, tiles, SUB, wide)] * QUARTERS,
        [full, full],
        state, *edges, north, ghosts, east,
        us=3.5,
    )
    pieces = to_longitudes(zs)
    (out,) = call(
        partial(unpack_kernel, tiles, direct), [sensitivity.shape], [(piece // 128, channels, 128)], *pieces
    )
    return out


def solution(mesh):
    return jax.shard_map(
        on_device,
        mesh=mesh,
        in_specs=(
            P("lat", "lon", None),
            P("lat", "lon", None),
            P("lat", "lon", None),
            P("lat", "lon", None),
            P("lat"),
            P("lat"),
        ),
        out_specs=P("lat", "lon", None),
        check_vma=False,
    )
```

```python
from functools import partial
import math

import jax
import jax.numpy as jnp
import ml_dtypes
import numpy as np
from jax import lax
from jax.experimental import pallas as pl
from jax.experimental.pallas import tpu as pltpu
from jax.sharding import PartitionSpec as P

SUBSTEPS = 2
QUARTERS = 4
HALO = 3
MIDDLE_ROOM = 16
PACK_US = 0.5
FILTER_US = 2.5
SUB = 8
f32 = jnp.float32
bf16 = jnp.bfloat16


def round_up(n, k):
    return -(-n // k) * k


def fourier_tables(nlon, wide):
    quarter = nlon // 4
    x = np.arange(2 * quarter)
    place = (x // quarter) * wide + x % quarter
    table = np.zeros((2, 2 * wide, round_up(quarter, 128)))
    for odd in (0, 1):
        k = np.arange(odd, quarter, 2)
        n = len(k)
        angle = (x[:, None] * k[None, :] % nlon) * (2.0 * math.pi / nlon)
        table[odd, place, :n] = np.cos(angle)
        table[odd, place, n : 2 * n] = np.sin(angle)
    high = table.astype(np.float32).astype(ml_dtypes.bfloat16)
    low = (table - high.astype(np.float64)).astype(np.float32).astype(ml_dtypes.bfloat16)
    return [high, low]


def wave_index(odd, count, shape):
    n = (count - odd + 1) // 2
    column = lax.broadcasted_iota(jnp.int32, shape, 1)
    wave = 2 * jnp.where(column < n, column, column - n) + odd
    return jnp.where(column < 2 * n, wave, 4 * count)


def split(x):
    high = x.astype(bf16)
    return high, (x - high.astype(f32)).astype(bf16)


def product(high, low, t_high, t_low, side):
    dot = lambda x, t: lax.dot_general(x, t, (((1,), (side,)), ((), ())), preferred_element_type=f32)
    n = high.shape[0]
    both = dot(jnp.concatenate([high, low], axis=0), t_high)
    return both[:n] + both[n:] + dot(high, t_low)


def column_factors(mix_at, levels, shape, store):
    zero = jnp.zeros(shape, f32)
    h_before = zero
    below = zero
    for level in range(levels):
        above = mix_at(level) if level < levels - 1 else zero
        divisor = 1.0 + below + above - below * h_before
        g = 1.0 / divisor
        h = above * g
        store(level, g, below * g, h)
        h_before = h
        below = above


def column_rest(h):
    n = len(h)
    before = lambda x: [pltpu.roll(x[n - 1], 1, 0)] + x[: n - 1]
    ratio = before(h)
    s = [jnp.ones(h[0].shape, f32)]
    carry = [ratio[0]]
    for q in range(1, n):
        s.append(1.0 + ratio[q] * s[q - 1])
        carry.append(ratio[q] * carry[q - 1])
    z, p = s[n - 1], carry[n - 1]
    step = 1
    while step < SUB:
        z = z + p * pltpu.roll(z, step, 0)
        if 2 * step < SUB:
            p = p * pltpu.roll(p, step, 0)
        step *= 2
    start = pltpu.roll(z, 1, 0)
    s = [s[q] + carry[q] * start for q in range(n - 1)] + [z]
    g = [(1.0 - h[q]) / s[q] for q in range(n)]
    mixing = before([h[q] * s[q] / (1.0 - h[q]) for q in range(n)])
    return g, [mixing[q] * g[q] for q in range(n)]


def column_solve(v, g, a, h):
    n = len(v)
    y = [g[0] * v[0]]
    carry = [a[0]]
    for q in range(1, n):
        y.append(g[q] * v[q] + a[q] * y[q - 1])
        carry.append(a[q] * carry[q - 1])
    z, p = y[n - 1], carry[n - 1]
    step = 1
    while step < SUB:
        z = z + p * pltpu.roll(z, step, 0)
        if 2 * step < SUB:
            p = p * pltpu.roll(p, step, 0)
        step *= 2
    before = pltpu.roll(z, 1, 0)
    y = [y[q] + carry[q] * before for q in range(n - 1)] + [z]
    x = [None] * n
    back = [None] * n
    x[n - 1] = y[n - 1]
    back[n - 1] = h[n - 1]
    for q in range(n - 2, -1, -1):
        x[q] = y[q] + h[q] * x[q + 1]
        back[q] = h[q] * back[q + 1]
    z, p = x[0], back[0]
    step = 1
    while step < SUB:
        z = z + p * pltpu.roll(z, SUB - step, 0)
        if 2 * step < SUB:
            p = p * pltpu.roll(p, SUB - step, 0)
        step *= 2
    after = pltpu.roll(z, SUB - 1, 0)
    return [z] + [x[q] + back[q] * after for q in range(1, n)]


def put(ref, at, value):
    for c in range(ref.shape[0]):
        n = min(128, value.shape[1] - c * 128)
        ref[c, at, :n] = value[:, c * 128 : c * 128 + n]


def get(ref, at):
    return jnp.concatenate([ref[c, at, :] for c in range(ref.shape[0])], axis=1)


def order_of(j, direct):
    return lax.axis_index("lon") ^ j if direct else j


def at_odd():
    return lax.axis_index("lat") % 2


def at_end(end):
    return lax.axis_index("lat") == (lax.axis_size("lat") - 1 if end else 0)


def clear(*refs):
    for ref in refs:
        ref[...] = jnp.zeros(ref.shape, f32)


def factor_scratch(rows, levels, wide):
    return [(wide // 128, rows * levels, 128)] * 3


def first_solve_kernel(tiles, direct, sens, mix, north, *refs):
    rows, width, channels = sens.shape
    levels = mix.shape[0] + 1
    tracers = channels // levels
    outs, h_out = refs[:tracers], refs[tracers]
    turned, packed, g_s, a_s, h_s, sens_v, mix_v, north_v, sems = refs[tracers + 1 :]
    loads = [pltpu.make_async_copy(mix, mix_v, sems.at[2 * rows])]
    loads += [pltpu.make_async_copy(sens.at[r], sens_v.at[r], sems.at[r]) for r in range(rows)]
    loads += [pltpu.make_async_copy(north.at[r], north_v.at[r], sems.at[rows + r]) for r in range(rows)]
    for load in loads:
        load.start()
    clear(turned, packed, g_s, a_s, h_s)
    loads[0].wait()

    def store(level, g, a, h):
        at = pl.ds((level % tiles) * SUB + level // tiles, rows, stride=levels)
        for s, value in ((g_s, g), (a_s, a), (h_s, h)):
            put(s, at, value)

    column_factors(lambda l: mix_v[l], levels, (rows, width), store)
    for r in range(rows):
        loads[1 + r].wait()
        put(turned, slice(0, channels), sens_v[r].T)
        at = lambda q: slice(r * levels + q * SUB, r * levels + q * SUB + SUB)
        g, a, h = ([get(s, at(q)) for q in range(tiles)] for s in (g_s, a_s, h_s))
        for q in range(tiles):
            h_out[r, q] = h[q]
        for j in range(tracers):
            t = order_of(j, direct)
            v = [get(turned, pl.ds(q * tracers + t, SUB, stride=tiles * tracers)) for q in range(tiles)]
            x = column_solve(v, g, a, h)
            for q in range(tiles):
                outs[j][r, q] = x[q]
    for r in range(rows):
        loads[1 + rows + r].wait()
        put(packed, slice(r * levels, (r + 1) * levels), north_v[r])
        for q in range(tiles):
            value = get(packed, pl.ds(r * levels + q, SUB, stride=tiles))
            for j in range(tracers):
                outs[j][rows + r, q] = value


def pack_both_kernel(tiles, h, *refs):
    src, out, src_v, turned, sems = refs[-5:]
    rows, levels, width = src.shape
    loads = [pltpu.make_async_copy(src.at[r], src_v.at[r], sems.at[r]) for r in range(rows)]
    for load in loads:
        load.start()
    clear(turned)
    for r in range(rows):
        for q in range(tiles):
            out[1, r * tiles + q] = h[r, q]
    for r in range(rows):
        loads[r].wait()
        put(turned, slice(r * levels, (r + 1) * levels), src_v[r])
        for q in range(tiles):
            out[0, r * tiles + q] = get(turned, pl.ds(r * levels + q, SUB, stride=tiles))


def unpack_kernel(tiles, direct, *refs):
    n = len(refs) - 2
    pieces, out, turned = refs[:n], refs[n], refs[n + 1]
    rows, width, channels = out.shape
    for r in range(rows):
        for j in range(n):
            t = order_of(j, direct)
            for q in range(tiles):
                put(turned, pl.ds(q * n + t, SUB, stride=tiles * n), pieces[j][r, q])
        out[r] = get(turned, slice(0, channels))[:, :width].T


def filter_block(count, field, tables, cut, flag, emit):
    rows, groups, sub, wide = field.shape
    tiles = groups // QUARTERS
    levels = tiles * sub
    quarter = [
        field[:, q * tiles : (q + 1) * tiles].reshape(rows * levels, wide) for q in range(QUARTERS)
    ]
    halves = []
    for sign in (0, 1):
        t_high, t_low = (t[sign] for t in tables)
        index = wave_index(sign, count, (levels, t_high.shape[1]))
        scale = jnp.where(index == 0, 1.0, 2.0) / (4 * count)
        if sign:
            pair = [quarter[0] - quarter[2], quarter[1] - quarter[3]]
        else:
            pair = [quarter[0] + quarter[2], quarter[1] + quarter[3]]
        high, low = split(jnp.concatenate(pair, axis=1))
        spectrum = product(high, low, t_high, t_low, 0)
        kept = [
            jnp.where(index <= cut(r), spectrum[r * levels : (r + 1) * levels] * scale, 0.0)
            for r in range(rows)
        ]
        high, low = split(jnp.concatenate(kept, axis=0))
        halves.append(product(high, low, t_high, t_low, 1))
    even, odd = halves
    for r in range(rows):
        at = slice(r * levels, (r + 1) * levels)
        for q in range(QUARTERS):
            lanes = slice((q % 2) * wide, (q % 2 + 1) * wide)
            e, o = even[at, lanes], odd[at, lanes]
            smooth = e + o if q < 2 else e - o
            emit(r, q, jnp.where(flag(r) > 0, smooth, quarter[q][at]))


def load_settings(cutoff, polar_flag, cut_s, flag_s, sems):
    loads = [pltpu.make_async_copy(cutoff, cut_s, sems.at[0]), pltpu.make_async_copy(polar_flag, flag_s, sems.at[1])]
    for load in loads:
        load.start()
    return loads


def settings_scratch(rows):
    return [pltpu.SMEM((rows,), jnp.int32)] * 2 + [pltpu.SemaphoreType.DMA((2,))]


def filter_and_edges(count, field, tables, cutoff, polar_flag, out, edge_z, edge_c):
    rows, groups, sub, wide = field.shape
    tiles = groups // QUARTERS
    active = polar_flag[0]
    for r in range(1, rows):
        active = active | polar_flag[r]

    @pl.when(active > 0)
    def _():
        def emit(r, q, value):
            out[r, q * tiles : (q + 1) * tiles] = value.reshape(tiles, sub, wide)

        filter_block(count, field, tables, lambda r: cutoff[r], lambda r: polar_flag[r], emit)

    @pl.when(active == 0)
    def _():
        out[...] = field[...]

    write_edges(out, edge_z, edge_c, 0)


def write_edges(field, edge_z, edge_c, at):
    shift = field.shape[0] - HALO
    odd = at_odd()
    edge_z[at : at + HALO] = field[pl.ds(odd * shift, HALO)]
    edge_c[at : at + HALO] = field[pl.ds((1 - odd) * shift, HALO)]


def by_parity(from_z, from_c, body):
    odd = at_odd()

    @pl.when(odd == 1)
    def _():
        body(from_c, from_z)

    @pl.when(odd == 0)
    def _():
        body(from_z, from_c)


def face_weights(courant):
    size = jnp.abs(courant)
    rest = 1.0 - size
    t = courant * rest
    edge = t * rest
    upwind = t * size
    cell = courant * size * (3.0 - 2.0 * size)
    ahead = courant >= 0.0
    small = (1.0 / 12.0) * upwind
    small_plus = jnp.where(ahead, small, 0.0)
    small_minus = small - small_plus
    near = (7.0 / 12.0) * edge
    far = (-1.0 / 12.0) * edge
    large = cell - 7.0 * small
    return {
        -2: small_plus,
        -1: far - 7.0 * small_plus,
        0: near + jnp.where(ahead, large, small),
        1: near + jnp.where(ahead, small, large),
        2: far - 7.0 * small_minus,
        3: small_minus,
    }


def stencil(before, now, m):
    if m == 3:
        return before
    if m == -3:
        return -now
    return before - now + 1.0 if m == 0 else before - now


def north_factors(courant, ghosts, out):
    rows, groups = out.shape[1:3]

    def body(i, _):
        before = None
        for f in range(-HALO, rows + HALO):
            now = face_weights(courant(f, i)) if f < rows + HALO - 1 else None
            for r in range(rows):
                m = f - r
                if -HALO <= m <= HALO:
                    out[m + HALO, r, i] = stencil(
                        before[1 - m] if m > -HALO else None, now[-m] if m < HALO else None, m
                    )
            for end, pole_face, step in ((0, 0, 1), (1, rows - 2, -1)):
                for face, k, slot in ((pole_face, 1, 0), (pole_face + step, 2, 1), (pole_face, 2, 2)):
                    if f == face:

                        @pl.when(at_end(end))
                        def _():
                            ghosts[slot, i] = now[k + 1 if end else -k]

            before = now
        return 0

    lax.fori_loop(0, groups, body, 0, unroll=4)


def meridional_pass(field, before, after, north, out):
    rows, groups, sub, wide = field.shape

    def body(i, _):
        total = [None] * rows
        for g in range(-HALO, rows + HALO):
            if g < 0:
                v = before[g + HALO, i]
            else:
                v = field[g, i] if g < rows else after[g - rows, i]
            for r in range(rows):
                if -HALO <= g - r <= HALO:
                    term = north[g - r + HALO, r, i] * v
                    total[r] = term if total[r] is None else total[r] + term
        for r in range(rows):
            out[r, i] = total[r]
        return 0

    lax.fori_loop(0, groups, body, 0, unroll=4)


def pole_pass(field, ghosts, out):
    rows, groups, sub, wide = out.shape
    half = groups // 2
    for end in (0, 1):

        @pl.when(at_end(end))
        def _():
            first, second, third = (rows - 1, rows - 2, rows - 3) if end else (0, 1, 2)

            def body(i, _):
                j = (i + half) % groups
                v0, v1, v2 = field[first, j], field[second, j], field[third, j]
                near = v0 - v1 if end else v1 - v0
                far = v1 - v2 if end else v2 - v1
                out[first, i] = out[first, i] + ghosts[0, j] * near + ghosts[1, j] * far
                out[second, i] = out[second, i] + ghosts[2, j] * near
                return 0

            lax.fori_loop(0, groups, body, 0, unroll=4)


def widen(values, width):
    wide = values[0].shape[1]
    lane = lax.broadcasted_iota(jnp.int32, values[0].shape, 1)
    result = []
    for q in range(QUARTERS):
        after = pltpu.roll(values[(q + 1) % QUARTERS], width, 1)
        before = pltpu.roll(values[(q - 1) % QUARTERS], wide - width, 1)
        padded = jnp.where(lane < width + HALO, after, before)
        padded = jnp.where((lane >= width + HALO) & (lane < wide - HALO), 0.0, padded)
        result.append(jnp.where(lane < width, values[q], padded))
    return result


def shifted(x, m):
    return x if m == 0 else pltpu.roll(x, -m % x.shape[1], 1)


def zonal_pass(width, field, east, emit):
    rows, groups, sub, wide = field.shape
    tiles = groups // QUARTERS

    def body(i, _):
        r, tile = i // tiles, i % tiles
        values = widen([field[r, q * tiles + tile] for q in range(QUARTERS)], width)
        for q in range(QUARTERS):
            total = None
            for m in range(-HALO, HALO + 1):
                term = east[m + HALO, r, q * tiles + tile] * shifted(values[q], m)
                total = term if total is None else total + term
            emit(r, q, tile, total)
        return 0

    lax.fori_loop(0, rows * tiles, body, 0, unroll=4)


def east_factors(width, courant, out):
    rows, groups, sub, wide = courant.shape
    tiles = groups // QUARTERS

    def body(i, _):
        r, tile = i // tiles, i % tiles
        values = widen([courant[r, q * tiles + tile] for q in range(QUARTERS)], width)
        for q in range(QUARTERS):
            w = {k: shifted(x, -k) for k, x in face_weights(values[q]).items()}
            for m in range(-HALO, HALO + 1):
                out[m + HALO, r, q * tiles + tile] = stencil(w.get(1 - m), w.get(-m), m)
        return 0

    lax.fori_loop(0, rows * tiles, body, 0, unroll=4)


def solve_pass(field, g, a, h):
    rows, groups, sub, wide = field.shape
    tiles = groups // QUARTERS

    def body(i, _):
        r, q = i // QUARTERS, i % QUARTERS
        take = lambda ref: [ref[r, q * tiles + tile] for tile in range(tiles)]
        x = column_solve(take(field), take(g), take(a), take(h))
        for tile in range(tiles):
            field[r, q * tiles + tile] = x[tile]
        return 0

    lax.fori_loop(0, rows * QUARTERS, body, 0, unroll=4)


def place(pieces, tiles, direct, out):
    for j in range(QUARTERS):
        out[:, pl.ds(order_of(j, direct) * tiles, tiles)] = pieces[j][...]


def first_filter_kernel(tiles, direct, count, *refs):
    pieces, tables = refs[:4], refs[4:6]
    cutoff, polar_flag, out, north, edge_z, edge_c, field, cut_s, flag_s, sems = refs[-10:]
    rows = field.shape[0]
    loads = load_settings(cutoff, polar_flag, cut_s, flag_s, sems)
    for j in range(QUARTERS):
        at = pl.ds(order_of(j, direct) * tiles, tiles)
        field[:, at] = pieces[j][:rows]
        north[:, at] = pieces[j][rows:]

    @pl.when(at_end(1))
    def _():
        north[rows - 1] = jnp.zeros(north.shape[1:], f32)

    write_edges(north, edge_z, edge_c, HALO)
    for load in loads:
        load.wait()
    filter_and_edges(count, field, tables, cut_s, flag_s, out, edge_z, edge_c)


def north_factor_kernel(north, from_z, from_c, *refs):
    out, ghosts = refs[-2:]
    rows = north.shape[0]

    def body(before, after):
        def courant(g, i):
            if g < 0:
                return before[HALO + g + HALO, i]
            return north[g, i] if g < rows else after[HALO + g - rows, i]

        north_factors(courant, ghosts, out)

    by_parity(from_z, from_c, body)


def east_factor_kernel(tiles, direct, width, *refs):
    pieces, out, raw = refs[:4], refs[-2], refs[-1]
    for j in range(QUARTERS):
        at = pl.ds(order_of(j, direct) * tiles, tiles)
        for r in range(raw.shape[0]):
            raw[r, at] = pieces[j][0, r * tiles : (r + 1) * tiles]
    east_factors(width, raw, out)


def column_factor_kernel(tiles, direct, *refs):
    pieces = refs[:4]
    g_o, a_o, h_o = refs[-3:]

    def body(r, _):
        for j in range(QUARTERS):
            h = [pieces[j][1, r * tiles + q] for q in range(tiles)]
            g, a = column_rest(h)
            for q in range(tiles):
                at = order_of(j, direct) * tiles + q
                g_o[r, at] = g[q]
                a_o[r, at] = a[q]
                h_o[r, at] = h[q]
        return 0

    lax.fori_loop(0, g_o.shape[0], body, 0)


def advect(width, field, from_z, from_c, north, ghosts, east, work, emit):
    by_parity(from_z, from_c, lambda before, after: meridional_pass(field, before, after, north, work))
    pole_pass(field, ghosts, work)
    zonal_pass(width, work, east, emit)


def middle_kernel(width, field, from_z, from_c, north, ghosts, east, g, a, h, *refs):
    tables = refs[:2]
    cutoff, polar_flag, out, edge_z, edge_c, work, result, cut_s, flag_s, sems = refs[2:]
    loads = load_settings(cutoff, polar_flag, cut_s, flag_s, sems)
    tiles = field.shape[1] // QUARTERS

    def emit(r, q, tile, value):
        result[r, q * tiles + tile] = value

    advect(width, field, from_z, from_c, north, ghosts, east, work, emit)
    solve_pass(result, g, a, h)
    for load in loads:
        load.wait()
    filter_and_edges(width, result, tables, cut_s, flag_s, out, edge_z, edge_c)


def last_kernel(width, direct, field, from_z, from_c, north, ghosts, east, *refs):
    outs = refs[:4]
    work, result = refs[4:]
    tiles = field.shape[1] // QUARTERS

    def emit(r, q, tile, value):
        result[r, q * tiles + tile] = value

    advect(width, field, from_z, from_c, north, ghosts, east, work, emit)
    for j in range(QUARTERS):
        outs[j][...] = result[:, pl.ds(order_of(j, direct) * tiles, tiles)]


def call(kernel, outs, scratch, *args, us=1.0, room=16, outside=()):
    specs = [pl.BlockSpec(memory_space=pltpu.VMEM)] * len(args)
    specs += [pl.BlockSpec(memory_space=pltpu.HBM)] * len(outside)
    outside = [pltpu.with_memory_space_constraint(x, pltpu.HBM) for x in outside]
    return pl.pallas_call(
        kernel,
        out_shape=[jax.ShapeDtypeStruct(s, f32) if isinstance(s, tuple) else s for s in outs],
        in_specs=specs,
        out_specs=[pl.BlockSpec(memory_space=pltpu.VMEM)] * len(outs),
        scratch_shapes=[pltpu.VMEM(s, f32) if isinstance(s, tuple) else s for s in scratch],
        compiler_params=pltpu.CompilerParams(vmem_limit_bytes=room * 2**20),
        cost_estimate=pl.CostEstimate(flops=int(us * 10**9), bytes_accessed=10**5, transcendentals=0),
    )(*args, *outside)


def nothing_kernel(*refs):
    pass


def held_until(x, *after):
    return pl.pallas_call(
        nothing_kernel,
        out_shape=jax.ShapeDtypeStruct(x.shape, x.dtype),
        in_specs=[pl.BlockSpec(memory_space=pltpu.VMEM)] * (1 + len(after)),
        out_specs=pl.BlockSpec(memory_space=pltpu.VMEM),
        input_output_aliases={0: 0},
        compiler_params=pltpu.CompilerParams(vmem_limit_bytes=16 * 2**20),
    )(x, *after)


def lat_exchange(edge_z, edge_c):
    count = lax.axis_size("lat")
    pairs = lambda start: [p for i in range(start, count - 1, 2) for p in ((i, i + 1), (i + 1, i))]
    from_z = lax.ppermute(edge_z, "lat", pairs(1))
    from_c = lax.ppermute(edge_c, "lat", pairs(0))
    return from_z, from_c


def on_device(sensitivity, courant_east, courant_north, mixing, cutoff, polar_flag):
    rows, width, channels = sensitivity.shape
    levels = courant_east.shape[2]
    tracers = channels // levels
    tiles = levels // SUB
    parts = lax.axis_size("lon")
    nlon = width * parts
    quarter = nlon // QUARTERS
    wide = round_up(quarter + 2 * HALO, 128)
    direct = parts == tracers == QUARTERS
    piece = wide if direct else round_up(width, 128)
    tables = fourier_tables(nlon, wide)

    swap = lambda x, s: lax.ppermute(x, "lon", [(i, i ^ s) for i in range(parts)])

    def quarters_of(blocks):
        whole = jnp.moveaxis(blocks[..., :width], 0, -2)
        whole = whole.reshape(whole.shape[:-2] + (QUARTERS, quarter))
        whole = jnp.pad(whole, [(0, 0)] * (whole.ndim - 1) + [(0, wide - quarter)])
        return [whole[..., q, :] for q in range(QUARTERS)]

    def gather(x):
        if direct:
            return [x] + [swap(x, s) for s in range(1, parts)]
        return quarters_of(lax.all_gather(x, "lon"))

    def to_tracers(ys):
        if direct:
            return [ys[0]] + [swap(ys[s], s) for s in range(1, parts)]
        sent = jnp.stack([ys[d % tracers] for d in range(parts)])
        return quarters_of(lax.all_to_all(sent, "lon", split_axis=0, concat_axis=0, tiled=True))

    def to_longitudes(zs):
        if direct:
            return [zs[0]] + [swap(zs[s], s) for s in range(1, parts)]
        whole = jnp.concatenate([z[..., :quarter] for z in zs], axis=-1)
        blocks = jnp.moveaxis(whole.reshape(whole.shape[:-1] + (parts, width)), -2, 0)
        came = lax.all_to_all(blocks, "lon", split_axis=0, concat_axis=0, tiled=True)
        came = jnp.pad(came, [(0, 0)] * (came.ndim - 1) + [(0, piece - width)])
        return [came[t] for t in range(tracers)]

    north_t = courant_north.transpose(0, 2, 1)
    east_t = courant_east.transpose(0, 2, 1)
    mix_t = mixing.transpose(2, 0, 1)
    block = (rows, tiles, SUB, piece)
    full = (rows, QUARTERS * tiles, SUB, wide)
    edge = (HALO,) + full[1:]
    turned = (piece // 128, rows * levels, 128)

    *ys, h_piece = call(
        partial(first_solve_kernel, tiles, direct),
        [(2 * rows,) + block[1:]] * tracers + [block],
        [(piece // 128, channels, 128), turned]
        + factor_scratch(rows, levels, piece)
        + [sensitivity.shape, mix_t.shape, north_t.shape, pltpu.SemaphoreType.DMA((2 * rows + 1,))],
        outside=[sensitivity, mix_t, north_t],
        us=3.0,
    )
    pieces = to_tracers(ys)
    (both,) = call(
        partial(pack_both_kernel, tiles),
        [(2, rows * tiles, SUB, piece)],
        [east_t.shape, turned, pltpu.SemaphoreType.DMA((rows,))],
        h_piece,
        outside=[east_t],
        us=PACK_US,
    )
    both = held_until(both, *pieces[1:])
    both_pieces = gather(both)
    both_edge = (2 * HALO,) + full[1:]
    state, north, edge_z, edge_c = call(
        partial(first_filter_kernel, tiles, direct, quarter),
        [full, full, both_edge, both_edge],
        [full] + settings_scratch(rows),
        *pieces, *tables, both,
        us=FILTER_US,
        outside=[cutoff, polar_flag],
    )
    edges = lat_exchange(edge_z, edge_c)
    (east,) = call(
        partial(east_factor_kernel, tiles, direct, quarter), [(2 * HALO + 1,) + full], [full], *both_pieces, us=10.0
    )
    g, a, h = call(
        partial(column_factor_kernel, tiles, direct),
        [full] * 3,
        [],
        *both_pieces,
        us=10.0,
    )
    north, ghosts = call(
        north_factor_kernel, [(2 * HALO + 1,) + full, (3,) + full[1:]], [], north, *edges, us=1.5
    )
    for substep in range(SUBSTEPS - 1):
        state, edge_z, edge_c = call(
            partial(middle_kernel, quarter),
            [full, edge, edge],
            [full, full] + settings_scratch(rows),
            state, *edges, north, ghosts, east, g, a, h, *tables,
            room=MIDDLE_ROOM,
        us=6.0,
            outside=[cutoff, polar_flag],
        )
        edges = lat_exchange(edge_z, edge_c)
    zs = call(
        partial(last_kernel, quarter, direct),
        [(rows, tiles, SUB, wide)] * QUARTERS,
        [full, full],
        state, *edges, north, ghosts, east,
        us=3.5,
    )
    pieces = to_longitudes(zs)
    (out,) = call(
        partial(unpack_kernel, tiles, direct), [sensitivity.shape], [(piece // 128, channels, 128)], *pieces
    )
    return out


def solution(mesh):
    return jax.shard_map(
        on_device,
        mesh=mesh,
        in_specs=(
            P("lat", "lon", None),
            P("lat", "lon", None),
            P("lat", "lon", None),
            P("lat", "lon", None),
            P("lat"),
            P("lat"),
        ),
        out_specs=P("lat", "lon", None),
        check_vma=False,
    )
```

```python
from functools import partial
import math

import jax
import jax.numpy as jnp
import ml_dtypes
import numpy as np
from jax import lax
from jax.experimental import pallas as pl
from jax.experimental.pallas import tpu as pltpu
from jax.sharding import PartitionSpec as P

SUBSTEPS = 2
QUARTERS = 4
HALO = 3
MIDDLE_ROOM = 16
PACK_US = 0.5
FILTER_US = 2.5
SUB = 8
f32 = jnp.float32
bf16 = jnp.bfloat16


def round_up(n, k):
    return -(-n // k) * k


def fourier_tables(nlon, wide):
    quarter = nlon // 4
    x = np.arange(2 * quarter)
    place = (x // quarter) * wide + x % quarter
    table = np.zeros((2, 2 * wide, round_up(quarter, 128)))
    for odd in (0, 1):
        k = np.arange(odd, quarter, 2)
        n = len(k)
        angle = (x[:, None] * k[None, :] % nlon) * (2.0 * math.pi / nlon)
        table[odd, place, :n] = np.cos(angle)
        table[odd, place, n : 2 * n] = np.sin(angle)
    high = table.astype(np.float32).astype(ml_dtypes.bfloat16)
    low = (table - high.astype(np.float64)).astype(np.float32).astype(ml_dtypes.bfloat16)
    return [high, low]


def wave_index(odd, count, shape):
    n = (count - odd + 1) // 2
    column = lax.broadcasted_iota(jnp.int32, shape, 1)
    wave = 2 * jnp.where(column < n, column, column - n) + odd
    return jnp.where(column < 2 * n, wave, 4 * count)


def split(x):
    high = x.astype(bf16)
    return high, (x - high.astype(f32)).astype(bf16)


def product(high, low, t_high, t_low, side):
    dot = lambda x, t: lax.dot_general(x, t, (((1,), (side,)), ((), ())), preferred_element_type=f32)
    n = high.shape[0]
    both = dot(jnp.concatenate([high, low], axis=0), t_high)
    return both[:n] + both[n:] + dot(high, t_low)


def column_factors(mix_at, levels, shape, store):
    zero = jnp.zeros(shape, f32)
    h_before = zero
    below = zero
    for level in range(levels):
        above = mix_at(level) if level < levels - 1 else zero
        divisor = 1.0 + below + above - below * h_before
        g = 1.0 / divisor
        h = above * g
        store(level, g, below * g, h)
        h_before = h
        below = above


def column_rest(h):
    n = len(h)
    before = lambda x: [pltpu.roll(x[n - 1], 1, 0)] + x[: n - 1]
    ratio = before(h)
    s = [jnp.ones(h[0].shape, f32)]
    carry = [ratio[0]]
    for q in range(1, n):
        s.append(1.0 + ratio[q] * s[q - 1])
        carry.append(ratio[q] * carry[q - 1])
    z, p = s[n - 1], carry[n - 1]
    step = 1
    while step < SUB:
        z = z + p * pltpu.roll(z, step, 0)
        if 2 * step < SUB:
            p = p * pltpu.roll(p, step, 0)
        step *= 2
    start = pltpu.roll(z, 1, 0)
    s = [s[q] + carry[q] * start for q in range(n - 1)] + [z]
    g = [(1.0 - h[q]) / s[q] for q in range(n)]
    mixing = before([h[q] * s[q] / (1.0 - h[q]) for q in range(n)])
    return g, [mixing[q] * g[q] for q in range(n)]


def column_solve(v, g, a, h):
    n = len(v)
    y = [g[0] * v[0]]
    carry = [a[0]]
    for q in range(1, n):
        y.append(g[q] * v[q] + a[q] * y[q - 1])
        carry.append(a[q] * carry[q - 1])
    z, p = y[n - 1], carry[n - 1]
    step = 1
    while step < SUB:
        z = z + p * pltpu.roll(z, step, 0)
        if 2 * step < SUB:
            p = p * pltpu.roll(p, step, 0)
        step *= 2
    before = pltpu.roll(z, 1, 0)
    y = [y[q] + carry[q] * before for q in range(n - 1)] + [z]
    x = [None] * n
    back = [None] * n
    x[n - 1] = y[n - 1]
    back[n - 1] = h[n - 1]
    for q in range(n - 2, -1, -1):
        x[q] = y[q] + h[q] * x[q + 1]
        back[q] = h[q] * back[q + 1]
    z, p = x[0], back[0]
    step = 1
    while step < SUB:
        z = z + p * pltpu.roll(z, SUB - step, 0)
        if 2 * step < SUB:
            p = p * pltpu.roll(p, SUB - step, 0)
        step *= 2
    after = pltpu.roll(z, SUB - 1, 0)
    return [z] + [x[q] + back[q] * after for q in range(1, n)]


def put(ref, at, value):
    for c in range(ref.shape[0]):
        n = min(128, value.shape[1] - c * 128)
        ref[c, at, :n] = value[:, c * 128 : c * 128 + n]


def get(ref, at):
    return jnp.concatenate([ref[c, at, :] for c in range(ref.shape[0])], axis=1)


def order_of(j, direct):
    return lax.axis_index("lon") ^ j if direct else j


def at_odd():
    return lax.axis_index("lat") % 2


def at_end(end):
    return lax.axis_index("lat") == (lax.axis_size("lat") - 1 if end else 0)


def clear(*refs):
    for ref in refs:
        ref[...] = jnp.zeros(ref.shape, f32)


def factor_scratch(rows, levels, wide):
    return [(wide // 128, rows * levels, 128)] * 3


def first_solve_kernel(tiles, direct, sens, mix, north, *refs):
    rows, width, channels = sens.shape
    levels = mix.shape[0] + 1
    tracers = channels // levels
    outs, h_out = refs[:tracers], refs[tracers]
    turned, packed, g_s, a_s, h_s, sens_v, mix_v, north_v, sems = refs[tracers + 1 :]
    loads = [pltpu.make_async_copy(mix, mix_v, sems.at[2 * rows])]
    loads += [pltpu.make_async_copy(sens.at[r], sens_v.at[r], sems.at[r]) for r in range(rows)]
    loads += [pltpu.make_async_copy(north.at[r], north_v.at[r], sems.at[rows + r]) for r in range(rows)]
    for load in loads:
        load.start()
    clear(turned, packed, g_s, a_s, h_s)
    loads[0].wait()

    def store(level, g, a, h):
        at = pl.ds((level % tiles) * SUB + level // tiles, rows, stride=levels)
        for s, value in ((g_s, g), (a_s, a), (h_s, h)):
            put(s, at, value)

    column_factors(lambda l: mix_v[l], levels, (rows, width), store)
    for r in range(rows):
        loads[1 + r].wait()
        put(turned, slice(0, channels), sens_v[r].T)
        at = lambda q: slice(r * levels + q * SUB, r * levels + q * SUB + SUB)
        g, a, h = ([get(s, at(q)) for q in range(tiles)] for s in (g_s, a_s, h_s))
        for q in range(tiles):
            h_out[r, q] = h[q]
        for j in range(tracers):
            t = order_of(j, direct)
            v = [get(turned, pl.ds(q * tracers + t, SUB, stride=tiles * tracers)) for q in range(tiles)]
            x = column_solve(v, g, a, h)
            for q in range(tiles):
                outs[j][r, q] = x[q]
    for r in range(rows):
        loads[1 + rows + r].wait()
        put(packed, slice(r * levels, (r + 1) * levels), north_v[r])
        for q in range(tiles):
            value = get(packed, pl.ds(r * levels + q, SUB, stride=tiles))
            for j in range(tracers):
                outs[j][rows + r, q] = value


def pack_both_kernel(tiles, h, *refs):
    src, out, src_v, turned, sems = refs[-5:]
    rows, levels, width = src.shape
    loads = [pltpu.make_async_copy(src.at[r], src_v.at[r], sems.at[r]) for r in range(rows)]
    for load in loads:
        load.start()
    clear(turned)
    for r in range(rows):
        for q in range(tiles):
            out[1, r * tiles + q] = h[r, q]
    for r in range(rows):
        loads[r].wait()
        put(turned, slice(r * levels, (r + 1) * levels), src_v[r])
        for q in range(tiles):
            out[0, r * tiles + q] = get(turned, pl.ds(r * levels + q, SUB, stride=tiles))


def unpack_kernel(tiles, direct, *refs):
    n = len(refs) - 2
    pieces, out, turned = refs[:n], refs[n], refs[n + 1]
    rows, width, channels = out.shape
    for r in range(rows):
        for j in range(n):
            t = order_of(j, direct)
            for q in range(tiles):
                put(turned, pl.ds(q * n + t, SUB, stride=tiles * n), pieces[j][r, q])
        out[r] = get(turned, slice(0, channels))[:, :width].T


def filter_block(count, field, tables, cut, flag, emit):
    rows, groups, sub, wide = field.shape
    tiles = groups // QUARTERS
    levels = tiles * sub
    quarter = [
        field[:, q * tiles : (q + 1) * tiles].reshape(rows * levels, wide) for q in range(QUARTERS)
    ]
    halves = []
    for sign in (0, 1):
        t_high, t_low = (t[sign] for t in tables)
        index = wave_index(sign, count, (levels, t_high.shape[1]))
        scale = jnp.where(index == 0, 1.0, 2.0) / (4 * count)
        if sign:
            pair = [quarter[0] - quarter[2], quarter[1] - quarter[3]]
        else:
            pair = [quarter[0] + quarter[2], quarter[1] + quarter[3]]
        high, low = split(jnp.concatenate(pair, axis=1))
        spectrum = product(high, low, t_high, t_low, 0)
        kept = [
            jnp.where(index <= cut(r), spectrum[r * levels : (r + 1) * levels] * scale, 0.0)
            for r in range(rows)
        ]
        high, low = split(jnp.concatenate(kept, axis=0))
        halves.append(product(high, low, t_high, t_low, 1))
    even, odd = halves
    for r in range(rows):
        at = slice(r * levels, (r + 1) * levels)
        for q in range(QUARTERS):
            lanes = slice((q % 2) * wide, (q % 2 + 1) * wide)
            e, o = even[at, lanes], odd[at, lanes]
            smooth = e + o if q < 2 else e - o
            emit(r, q, jnp.where(flag(r) > 0, smooth, quarter[q][at]))


def load_settings(cutoff, polar_flag, cut_s, flag_s, sems):
    loads = [pltpu.make_async_copy(cutoff, cut_s, sems.at[0]), pltpu.make_async_copy(polar_flag, flag_s, sems.at[1])]
    for load in loads:
        load.start()
    return loads


def settings_scratch(rows):
    return [pltpu.SMEM((rows,), jnp.int32)] * 2 + [pltpu.SemaphoreType.DMA((2,))]


def filter_and_edges(count, field, tables, cutoff, polar_flag, out, edge_z, edge_c):
    rows, groups, sub, wide = field.shape
    tiles = groups // QUARTERS
    active = polar_flag[0]
    for r in range(1, rows):
        active = active | polar_flag[r]

    @pl.when(active > 0)
    def _():
        def emit(r, q, value):
            out[r, q * tiles : (q + 1) * tiles] = value.reshape(tiles, sub, wide)

        filter_block(count, field, tables, lambda r: cutoff[r], lambda r: polar_flag[r], emit)

    @pl.when(active == 0)
    def _():
        out[...] = field[...]

    write_edges(out, edge_z, edge_c, 0)


def write_edges(field, edge_z, edge_c, at):
    shift = field.shape[0] - HALO
    odd = at_odd()
    edge_z[at : at + HALO] = field[pl.ds(odd * shift, HALO)]
    edge_c[at : at + HALO] = field[pl.ds((1 - odd) * shift, HALO)]


def by_parity(from_z, from_c, body):
    odd = at_odd()

    @pl.when(odd == 1)
    def _():
        body(from_c, from_z)

    @pl.when(odd == 0)
    def _():
        body(from_z, from_c)


def face_weights(courant):
    size = jnp.abs(courant)
    rest = 1.0 - size
    t = courant * rest
    edge = t * rest
    upwind = t * size
    cell = courant * size * (3.0 - 2.0 * size)
    ahead = courant >= 0.0
    small = (1.0 / 12.0) * upwind
    small_plus = jnp.where(ahead, small, 0.0)
    small_minus = small - small_plus
    near = (7.0 / 12.0) * edge
    far = (-1.0 / 12.0) * edge
    large = cell - 7.0 * small
    return {
        -2: small_plus,
        -1: far - 7.0 * small_plus,
        0: near + jnp.where(ahead, large, small),
        1: near + jnp.where(ahead, small, large),
        2: far - 7.0 * small_minus,
        3: small_minus,
    }


def stencil(before, now, m):
    if m == 3:
        return before
    if m == -3:
        return -now
    return before - now + 1.0 if m == 0 else before - now


def north_factors(courant, ghosts, out):
    rows, groups = out.shape[1:3]

    def body(i, _):
        before = None
        for f in range(-HALO, rows + HALO):
            now = face_weights(courant(f, i)) if f < rows + HALO - 1 else None
            for r in range(rows):
                m = f - r
                if -HALO <= m <= HALO:
                    out[m + HALO, r, i] = stencil(
                        before[1 - m] if m > -HALO else None, now[-m] if m < HALO else None, m
                    )
            for end, pole_face, step in ((0, 0, 1), (1, rows - 2, -1)):
                for face, k, slot in ((pole_face, 1, 0), (pole_face + step, 2, 1), (pole_face, 2, 2)):
                    if f == face:

                        @pl.when(at_end(end))
                        def _():
                            ghosts[slot, i] = now[k + 1 if end else -k]

            before = now
        return 0

    lax.fori_loop(0, groups, body, 0, unroll=4)


def meridional_pass(field, before, after, north, out):
    rows, groups, sub, wide = field.shape

    def body(i, _):
        total = [None] * rows
        for g in range(-HALO, rows + HALO):
            if g < 0:
                v = before[g + HALO, i]
            else:
                v = field[g, i] if g < rows else after[g - rows, i]
            for r in range(rows):
                if -HALO <= g - r <= HALO:
                    term = north[g - r + HALO, r, i] * v
                    total[r] = term if total[r] is None else total[r] + term
        for r in range(rows):
            out[r, i] = total[r]
        return 0

    lax.fori_loop(0, groups, body, 0, unroll=4)


def pole_pass(field, ghosts, out):
    rows, groups, sub, wide = out.shape
    half = groups // 2
    for end in (0, 1):

        @pl.when(at_end(end))
        def _():
            first, second, third = (rows - 1, rows - 2, rows - 3) if end else (0, 1, 2)

            def body(i, _):
                j = (i + half) % groups
                v0, v1, v2 = field[first, j], field[second, j], field[third, j]
                near = v0 - v1 if end else v1 - v0
                far = v1 - v2 if end else v2 - v1
                out[first, i] = out[first, i] + ghosts[0, j] * near + ghosts[1, j] * far
                out[second, i] = out[second, i] + ghosts[2, j] * near
                return 0

            lax.fori_loop(0, groups, body, 0, unroll=4)


def widen(values, width):
    wide = values[0].shape[1]
    lane = lax.broadcasted_iota(jnp.int32, values[0].shape, 1)
    result = []
    for q in range(QUARTERS):
        after = pltpu.roll(values[(q + 1) % QUARTERS], width, 1)
        before = pltpu.roll(values[(q - 1) % QUARTERS], wide - width, 1)
        padded = jnp.where(lane < width + HALO, after, before)
        padded = jnp.where((lane >= width + HALO) & (lane < wide - HALO), 0.0, padded)
        result.append(jnp.where(lane < width, values[q], padded))
    return result


def shifted(x, m):
    return x if m == 0 else pltpu.roll(x, -m % x.shape[1], 1)


def zonal_pass(width, field, east, emit):
    rows, groups, sub, wide = field.shape
    tiles = groups // QUARTERS

    def body(i, _):
        r, tile = i // tiles, i % tiles
        values = widen([field[r, q * tiles + tile] for q in range(QUARTERS)], width)
        for q in range(QUARTERS):
            total = None
            for m in range(-HALO, HALO + 1):
                term = east[m + HALO, r, q * tiles + tile] * shifted(values[q], m)
                total = term if total is None else total + term
            emit(r, q, tile, total)
        return 0

    lax.fori_loop(0, rows * tiles, body, 0, unroll=4)


def east_factors(width, courant, out):
    rows, groups, sub, wide = courant.shape
    tiles = groups // QUARTERS

    def body(i, _):
        r, tile = i // tiles, i % tiles
        values = widen([courant[r, q * tiles + tile] for q in range(QUARTERS)], width)
        for q in range(QUARTERS):
            w = {k: shifted(x, -k) for k, x in face_weights(values[q]).items()}
            for m in range(-HALO, HALO + 1):
                out[m + HALO, r, q * tiles + tile] = stencil(w.get(1 - m), w.get(-m), m)
        return 0

    lax.fori_loop(0, rows * tiles, body, 0, unroll=4)


def solve_pass(field, g, a, h):
    rows, groups, sub, wide = field.shape
    tiles = groups // QUARTERS

    def body(i, _):
        r, q = i // QUARTERS, i % QUARTERS
        take = lambda ref: [ref[r, q * tiles + tile] for tile in range(tiles)]
        x = column_solve(take(field), take(g), take(a), take(h))
        for tile in range(tiles):
            field[r, q * tiles + tile] = x[tile]
        return 0

    lax.fori_loop(0, rows * QUARTERS, body, 0, unroll=4)


def place(pieces, tiles, direct, out):
    for j in range(QUARTERS):
        out[:, pl.ds(order_of(j, direct) * tiles, tiles)] = pieces[j][...]


def first_filter_kernel(tiles, direct, count, *refs):
    pieces, tables = refs[:4], refs[4:6]
    cutoff, polar_flag, out, north, edge_z, edge_c, field, cut_s, flag_s, sems = refs[-10:]
    rows = field.shape[0]
    loads = load_settings(cutoff, polar_flag, cut_s, flag_s, sems)
    for j in range(QUARTERS):
        at = pl.ds(order_of(j, direct) * tiles, tiles)
        field[:, at] = pieces[j][:rows]
        north[:, at] = pieces[j][rows:]

    @pl.when(at_end(1))
    def _():
        north[rows - 1] = jnp.zeros(north.shape[1:], f32)

    write_edges(north, edge_z, edge_c, HALO)
    for load in loads:
        load.wait()
    filter_and_edges(count, field, tables, cut_s, flag_s, out, edge_z, edge_c)


def north_factor_kernel(north, from_z, from_c, *refs):
    out, ghosts = refs[-2:]
    rows = north.shape[0]

    def body(before, after):
        def courant(g, i):
            if g < 0:
                return before[HALO + g + HALO, i]
            return north[g, i] if g < rows else after[HALO + g - rows, i]

        north_factors(courant, ghosts, out)

    by_parity(from_z, from_c, body)


def east_factor_kernel(tiles, direct, width, *refs):
    pieces, out, raw = refs[:4], refs[-2], refs[-1]
    for j in range(QUARTERS):
        at = pl.ds(order_of(j, direct) * tiles, tiles)
        for r in range(raw.shape[0]):
            raw[r, at] = pieces[j][0, r * tiles : (r + 1) * tiles]
    east_factors(width, raw, out)


def column_factor_kernel(tiles, direct, *refs):
    pieces = refs[:4]
    g_o, a_o, h_o = refs[-3:]

    def body(r, _):
        for j in range(QUARTERS):
            h = [pieces[j][1, r * tiles + q] for q in range(tiles)]
            g, a = column_rest(h)
            for q in range(tiles):
                at = order_of(j, direct) * tiles + q
                g_o[r, at] = g[q]
                a_o[r, at] = a[q]
                h_o[r, at] = h[q]
        return 0

    lax.fori_loop(0, g_o.shape[0], body, 0)


def advect(width, field, from_z, from_c, north, ghosts, east, work, emit):
    by_parity(from_z, from_c, lambda before, after: meridional_pass(field, before, after, north, work))
    pole_pass(field, ghosts, work)
    zonal_pass(width, work, east, emit)


def middle_kernel(width, field, from_z, from_c, north, ghosts, east, g, a, h, *refs):
    tables = refs[:2]
    cutoff, polar_flag, out, edge_z, edge_c, work, result, cut_s, flag_s, sems = refs[2:]
    loads = load_settings(cutoff, polar_flag, cut_s, flag_s, sems)
    tiles = field.shape[1] // QUARTERS

    def emit(r, q, tile, value):
        result[r, q * tiles + tile] = value

    advect(width, field, from_z, from_c, north, ghosts, east, work, emit)
    solve_pass(result, g, a, h)
    for load in loads:
        load.wait()
    filter_and_edges(width, result, tables, cut_s, flag_s, out, edge_z, edge_c)


def last_kernel(width, direct, field, from_z, from_c, north, ghosts, east, *refs):
    outs = refs[:4]
    work, result = refs[4:]
    tiles = field.shape[1] // QUARTERS

    def emit(r, q, tile, value):
        result[r, q * tiles + tile] = value

    advect(width, field, from_z, from_c, north, ghosts, east, work, emit)
    for j in range(QUARTERS):
        outs[j][...] = result[:, pl.ds(order_of(j, direct) * tiles, tiles)]


def call(kernel, outs, scratch, *args, us=1.0, room=16, outside=()):
    specs = [pl.BlockSpec(memory_space=pltpu.VMEM)] * len(args)
    specs += [pl.BlockSpec(memory_space=pltpu.HBM)] * len(outside)
    outside = [pltpu.with_memory_space_constraint(x, pltpu.HBM) for x in outside]
    return pl.pallas_call(
        kernel,
        out_shape=[jax.ShapeDtypeStruct(s, f32) if isinstance(s, tuple) else s for s in outs],
        in_specs=specs,
        out_specs=[pl.BlockSpec(memory_space=pltpu.VMEM)] * len(outs),
        scratch_shapes=[pltpu.VMEM(s, f32) if isinstance(s, tuple) else s for s in scratch],
        compiler_params=pltpu.CompilerParams(vmem_limit_bytes=room * 2**20),
        cost_estimate=pl.CostEstimate(flops=int(us * 10**9), bytes_accessed=10**5, transcendentals=0),
    )(*args, *outside)


def nothing_kernel(*refs):
    pass


def held_until(x, *after):
    return pl.pallas_call(
        nothing_kernel,
        out_shape=jax.ShapeDtypeStruct(x.shape, x.dtype),
        in_specs=[pl.BlockSpec(memory_space=pltpu.VMEM)] * (1 + len(after)),
        out_specs=pl.BlockSpec(memory_space=pltpu.VMEM),
        input_output_aliases={0: 0},
        compiler_params=pltpu.CompilerParams(vmem_limit_bytes=16 * 2**20),
    )(x, *after)


def lat_exchange(edge_z, edge_c):
    count = lax.axis_size("lat")
    pairs = lambda start: [p for i in range(start, count - 1, 2) for p in ((i, i + 1), (i + 1, i))]
    from_z = lax.ppermute(edge_z, "lat", pairs(1))
    from_c = lax.ppermute(edge_c, "lat", pairs(0))
    return from_z, from_c


def on_device(sensitivity, courant_east, courant_north, mixing, cutoff, polar_flag):
    rows, width, channels = sensitivity.shape
    levels = courant_east.shape[2]
    tracers = channels // levels
    tiles = levels // SUB
    parts = lax.axis_size("lon")
    nlon = width * parts
    quarter = nlon // QUARTERS
    wide = round_up(quarter + 2 * HALO, 128)
    direct = parts == tracers == QUARTERS
    piece = wide if direct else round_up(width, 128)
    tables = fourier_tables(nlon, wide)

    swap = lambda x, s: lax.ppermute(x, "lon", [(i, i ^ s) for i in range(parts)])

    def quarters_of(blocks):
        whole = jnp.moveaxis(blocks[..., :width], 0, -2)
        whole = whole.reshape(whole.shape[:-2] + (QUARTERS, quarter))
        whole = jnp.pad(whole, [(0, 0)] * (whole.ndim - 1) + [(0, wide - quarter)])
        return [whole[..., q, :] for q in range(QUARTERS)]

    def gather(x):
        if direct:
            return [x] + [swap(x, s) for s in range(1, parts)]
        return quarters_of(lax.all_gather(x, "lon"))

    def to_tracers(ys):
        if direct:
            return [ys[0]] + [swap(ys[s], s) for s in range(1, parts)]
        sent = jnp.stack([ys[d % tracers] for d in range(parts)])
        return quarters_of(lax.all_to_all(sent, "lon", split_axis=0, concat_axis=0, tiled=True))

    def to_longitudes(zs):
        if direct:
            return [zs[0]] + [swap(zs[s], s) for s in range(1, parts)]
        whole = jnp.concatenate([z[..., :quarter] for z in zs], axis=-1)
        blocks = jnp.moveaxis(whole.reshape(whole.shape[:-1] + (parts, width)), -2, 0)
        came = lax.all_to_all(blocks, "lon", split_axis=0, concat_axis=0, tiled=True)
        came = jnp.pad(came, [(0, 0)] * (came.ndim - 1) + [(0, piece - width)])
        return [came[t] for t in range(tracers)]

    north_t = courant_north.transpose(0, 2, 1)
    east_t = courant_east.transpose(0, 2, 1)
    mix_t = mixing.transpose(2, 0, 1)
    block = (rows, tiles, SUB, piece)
    full = (rows, QUARTERS * tiles, SUB, wide)
    edge = (HALO,) + full[1:]
    turned = (piece // 128, rows * levels, 128)

    *ys, h_piece = call(
        partial(first_solve_kernel, tiles, direct),
        [(2 * rows,) + block[1:]] * tracers + [block],
        [(piece // 128, channels, 128), turned]
        + factor_scratch(rows, levels, piece)
        + [sensitivity.shape, mix_t.shape, north_t.shape, pltpu.SemaphoreType.DMA((2 * rows + 1,))],
        outside=[sensitivity, mix_t, north_t],
        us=3.0,
    )
    pieces = to_tracers(ys)
    (both,) = call(
        partial(pack_both_kernel, tiles),
        [(2, rows * tiles, SUB, piece)],
        [east_t.shape, turned, pltpu.SemaphoreType.DMA((rows,))],
        h_piece,
        outside=[east_t],
        us=PACK_US,
    )
    both = held_until(both, *pieces[1:])
    both_pieces = gather(both)
    both_edge = (2 * HALO,) + full[1:]
    state, north, edge_z, edge_c = call(
        partial(first_filter_kernel, tiles, direct, quarter),
        [full, full, both_edge, both_edge],
        [full] + settings_scratch(rows),
        *pieces, *tables, both,
        us=FILTER_US,
        outside=[cutoff, polar_flag],
    )
    edges = lat_exchange(edge_z, edge_c)
    (east,) = call(
        partial(east_factor_kernel, tiles, direct, quarter), [(2 * HALO + 1,) + full], [full], *both_pieces, us=10.0
    )
    g, a, h = call(
        partial(column_factor_kernel, tiles, direct),
        [full] * 3,
        [],
        *both_pieces,
        us=10.0,
    )
    north, ghosts = call(
        north_factor_kernel, [(2 * HALO + 1,) + full, (3,) + full[1:]], [], north, *edges, us=0.2
    )
    for substep in range(SUBSTEPS - 1):
        state, edge_z, edge_c = call(
            partial(middle_kernel, quarter),
            [full, edge, edge],
            [full, full] + settings_scratch(rows),
            state, *edges, north, ghosts, east, g, a, h, *tables,
            room=MIDDLE_ROOM,
        us=6.0,
            outside=[cutoff, polar_flag],
        )
        edges = lat_exchange(edge_z, edge_c)
    zs = call(
        partial(last_kernel, quarter, direct),
        [(rows, tiles, SUB, wide)] * QUARTERS,
        [full, full],
        state, *edges, north, ghosts, east,
        us=3.5,
    )
    pieces = to_longitudes(zs)
    (out,) = call(
        partial(unpack_kernel, tiles, direct), [sensitivity.shape], [(piece // 128, channels, 128)], *pieces
    )
    return out


def solution(mesh):
    return jax.shard_map(
        on_device,
        mesh=mesh,
        in_specs=(
            P("lat", "lon", None),
            P("lat", "lon", None),
            P("lat", "lon", None),
            P("lat", "lon", None),
            P("lat"),
            P("lat"),
        ),
        out_specs=P("lat", "lon", None),
        check_vma=False,
    )
```
